256 devices in a mesh: dp: 32 (over y, z_hi, core), expert: 8 (over z_lo, x).
Axes of the slice: x: 4, y: 4, z: 8 (z_hi: 4, z_lo: 2; z = z_hi * 2 + z_lo), core: 2. Of those that a mesh axis runs over, the one named last changes fastest.
Arguments:
- tokens: bfloat16 [512, 256, 1280], P(('dp', 'expert')), may hold values from -6 to 6
- grad_out: bfloat16 [512, 256, 1280], P(('dp', 'expert')), may hold values from -3 to 3
- logits: float32 [512, 32, 256], P(('dp', 'expert')), may hold values from -320 to 320
- router: bfloat16 [32, 1280], replicated, may hold values from -0.15625 to 0.15625
- fc1_out: bfloat16 [32, 512, 5120], P('dp', None, 'expert'), may hold values from -6 to 6
- w_in: bfloat16 [32, 1280, 5120], P('dp', None, 'expert'), may hold values from -0.15625 to 0.15625
- w_out: bfloat16 [32, 5120, 1280], P('dp', 'expert'), may hold values from -0.078125 to 0.078125
Outputs:
- grad_tokens: bfloat16 [512, 256, 1280], P(('dp', 'expert'))
- grad_router: float32 [32, 1280], replicated
- grad_w_in: bfloat16 [32, 1280, 5120], P('dp', None, 'expert')
- grad_w_out: bfloat16 [32, 5120, 1280], P('dp', 'expert')
The draws below stay inside these ranges and needn't reach their ends.
All inputs are finite; a program needn't handle non-finite values.
Results may differ from the reference program's by a relative error of at most 0.02.
Values may be sent and summed in bfloat16 or wider, within the bound.
No kernel may reach another device: no remote copies, remote signals or barrier semaphores. Data moves between devices by JAX's collectives and lax.ppermute only.
A program may use at most 64 MiB of HBM per device.

```python
import jax
import jax.numpy as jnp
from jax import lax

D = 1280
FF = 5120
M = 256
EXPERTS = 32
IMAGES = 512
N_EXPERT = 8


def draw_logits(key, part):
    key = jax.random.fold_in(key, 11)
    key_base = jax.random.fold_in(key, 0)
    scores = jnp.clip(jax.random.normal(key_base, (IMAGES, EXPERTS, M), jnp.float32) * 3.0, -12.0, 12.0)
    return scores


def block_levels(key, shape, pieces, least, top_value):
    def one(axis_at, shards_of):
        draws = jax.random.uniform(jax.random.fold_in(jax.random.fold_in(key, 6), axis_at), (shards_of,), jnp.float32, least / len(pieces), top_value / len(pieces))
        return jnp.repeat(jnp.exp(draws), shape[axis_at] // shards_of).reshape((-1,) + (1,) * (len(shape) - axis_at - 1))

    factor_of = one(*pieces[0])
    for cut in pieces[1:]:
        factor_of = factor_of * one(*cut)
    return factor_of


def noise(stream_key, shape, deviation, limit, cuts=(), dtype=jnp.bfloat16):
    result = deviation * jax.random.normal(stream_key, shape, jnp.float32)
    if cuts:
        result = result * block_levels(stream_key, shape, cuts, -0.22, 0.18)
    return jnp.clip(result, -limit, limit).astype(dtype)


def setup_inputs(seed: int = 0) -> dict:
    keys = jax.random.split(jax.random.key(seed), 8)
    tokens = noise(keys[0], (IMAGES, M, D), 1.0, 6.0, ((0, 256),))
    grad_out = noise(keys[1], (IMAGES, M, D), 0.5, 3.0, ((0, 256),))
    logits = draw_logits(jax.random.fold_in(keys[7], 71), 0)
    router = noise(keys[3], (EXPERTS, D), D ** -0.5, 0.15625)
    fc1_out = noise(keys[4], (EXPERTS, IMAGES, FF), 1.0, 6.0, ((0, 32), (2, 8)))
    w_in = noise(keys[5], (EXPERTS, D, FF), D ** -0.5, 0.15625, ((0, 32), (2, 8)))
    w_out = noise(keys[6], (EXPERTS, FF, D), FF ** -0.5, 0.078125, ((0, 32), (1, 8)))
    return {"tokens": tokens, "grad_out": grad_out, "logits": logits, "router": router, "fc1_out": fc1_out, "w_in": w_in, "w_out": w_out}


def gelu_slope(value):
    cdf = 0.5 * (1.0 + jax.scipy.special.erf(value * 0.7071067811865476))
    density = jnp.exp(-0.5 * value * value) * 0.3989422804014327
    return cdf + value * density


def soft_weights(scores):
    over_tokens = jnp.exp(scores - jnp.max(scores, axis=1, keepdims=True))
    disp = over_tokens / jnp.sum(over_tokens, axis=1, keepdims=True)
    over_slots = jnp.exp(scores - jnp.max(scores, axis=0, keepdims=True))
    comb = over_slots / jnp.sum(over_slots, axis=0, keepdims=True)
    return disp, comb


def block_sum(parts):
    rounded = lax.optimization_barrier(parts.astype(jnp.bfloat16))
    return jnp.sum(rounded.astype(jnp.float32), axis=0).astype(jnp.bfloat16)


def reference(tokens, grad_out, logits, router, fc1_out, w_in, w_out):
    def forward_image(item):
        x_rows, dy_rows, scores = item
        disp, comb = soft_weights(scores)
        slot_in = jnp.dot(disp.astype(jnp.bfloat16), x_rows, preferred_element_type=jnp.float32).astype(jnp.bfloat16)
        slot_grad = jnp.dot(comb.astype(jnp.bfloat16), dy_rows, preferred_element_type=jnp.float32).astype(jnp.bfloat16)
        return slot_in, slot_grad

    slot_in, slot_grad = lax.map(forward_image, (tokens, grad_out, logits))
    slot_in_e = jnp.transpose(slot_in, (1, 0, 2))
    slot_grad_e = jnp.transpose(slot_grad, (1, 0, 2))
    shard = FF // N_EXPERT

    def expert(item):
        pre, first, second, x_slots, dy_slots = item
        pre_f = pre.astype(jnp.float32)
        act = jax.nn.gelu(pre_f, approximate=False).astype(jnp.bfloat16)
        act3 = act.astype(jnp.float32).reshape(IMAGES, N_EXPERT, shard)
        second3 = second.astype(jnp.float32).reshape(N_EXPERT, shard, D)
        parts = jnp.einsum("rkf,kfd->krd", act3, second3, precision=lax.Precision.HIGHEST)
        slot_out = block_sum(parts)
        act_grad = jnp.dot(dy_slots, second.T, preferred_element_type=jnp.float32)
        hid_grad = (act_grad * gelu_slope(pre_f)).astype(jnp.bfloat16)
        grad_second = jnp.dot(act.T, dy_slots, preferred_element_type=jnp.float32).astype(jnp.bfloat16)
        grad_first = jnp.dot(x_slots.T, hid_grad, preferred_element_type=jnp.float32).astype(jnp.bfloat16)
        hid3 = hid_grad.astype(jnp.float32).reshape(IMAGES, N_EXPERT, shard)
        first3 = first.astype(jnp.float32).reshape(D, N_EXPERT, shard)
        parts_back = jnp.einsum("rkf,dkf->krd", hid3, first3, precision=lax.Precision.HIGHEST)
        slot_in_grad = block_sum(parts_back)
        return slot_out, slot_in_grad, grad_first, grad_second

    slot_out, slot_in_grad, grad_w_in, grad_w_out = lax.map(expert, (fc1_out, w_in, w_out, slot_in_e, slot_grad_e))
    slot_out = jnp.transpose(slot_out, (1, 0, 2))
    slot_in_grad = jnp.transpose(slot_in_grad, (1, 0, 2))

    def backward_image(item):
        x_rows, dy_rows, scores, outs_b, back_b = item
        disp, comb = soft_weights(scores)
        comb_grad = jnp.dot(outs_b, dy_rows.T, preferred_element_type=jnp.float32)
        disp_grad = jnp.dot(back_b, x_rows.T, preferred_element_type=jnp.float32)
        through_comb = comb * (comb_grad - jnp.sum(comb * comb_grad, axis=0, keepdims=True))
        through_disp = disp * (disp_grad - jnp.sum(disp * disp_grad, axis=1, keepdims=True))
        logit_grad = (through_comb + through_disp).astype(jnp.bfloat16)
        grad_x = jnp.dot(disp.astype(jnp.bfloat16).T, back_b, preferred_element_type=jnp.float32)
        grad_x = grad_x + jnp.dot(logit_grad.T, router, preferred_element_type=jnp.float32)
        grad_r = jnp.dot(logit_grad, x_rows, preferred_element_type=jnp.float32)
        return grad_x.astype(jnp.bfloat16), grad_r

    grad_tokens, router_parts = lax.map(backward_image, (tokens, grad_out, logits, slot_out, slot_in_grad))
    grad_router = jnp.sum(router_parts, axis=0)
    return grad_tokens, grad_router, grad_w_in, grad_w_out
```

```python
import jax
import jax.numpy as jnp
from jax import lax
from jax.sharding import PartitionSpec as P

BF = jnp.bfloat16
F32 = jnp.float32


def gelu_slope(value):
    cdf = 0.5 * (1.0 + jax.scipy.special.erf(value * 0.7071067811865476))
    density = jnp.exp(-0.5 * value * value) * 0.3989422804014327
    return cdf + value * density


def dot(a, b, dims):
    return lax.dot_general(a, b, (dims, ((), ())), preferred_element_type=F32)


def exchange(blocks, axis):
    return lax.all_to_all(blocks, axis, split_axis=0, concat_axis=0, tiled=True)


def side_by_side(parts):
    return jnp.concatenate(parts, axis=1)


def on_device(tokens, grad_out, logits, router, fc1_out, w_in, w_out):
    images, slots, _ = logits.shape
    width = tokens.shape[2]
    dp_count = lax.axis_size("dp")
    ex_count = lax.axis_size("expert")
    group = dp_count * ex_count
    w_in, w_out, pre = w_in[0], w_out[0], fc1_out[0]

    over_slots = jnp.exp(logits - jnp.max(logits, axis=1, keepdims=True))
    comb = over_slots / jnp.sum(over_slots, axis=1, keepdims=True)
    comb_b = comb.astype(BF)
    over_tokens = jnp.exp(logits - jnp.max(logits, axis=2, keepdims=True))
    disp = over_tokens / jnp.sum(over_tokens, axis=2, keepdims=True)
    disp_b = disp.astype(BF)

    slot_grad = side_by_side([dot(comb_b[b], grad_out[b], ((1,), (0,))).astype(BF) for b in range(images)])
    slot_in = side_by_side([dot(disp_b[b], tokens[b], ((1,), (0,))).astype(BF) for b in range(images)])

    hidden = pre.shape[1]
    pre = pre.reshape(dp_count, ex_count, images, hidden).transpose(2, 1, 0, 3).reshape(-1, hidden)
    pre_f = pre.astype(F32)
    act = jax.nn.gelu(pre_f, approximate=False).astype(BF)
    slope = gelu_slope(pre_f)

    def by_image(rows):
        return jnp.concatenate([rows[:, b * width : (b + 1) * width] for b in range(images)], axis=0)

    def by_lane(rows):
        return side_by_side([rows[b * group : (b + 1) * group] for b in range(images)])

    moved_grad = exchange(slot_grad, "dp")
    all_grad = exchange(jnp.broadcast_to(moved_grad[None], (ex_count,) + moved_grad.shape), "expert")
    all_grad = by_image(all_grad.reshape(group, -1))

    out_part = by_lane(dot(act, w_out, ((1,), (0,))).astype(BF))
    out_sum = lax.psum_scatter(out_part, "expert", scatter_dimension=0, tiled=True)

    act_grad = dot(all_grad, w_out, ((1,), (1,)))
    hid_grad = (act_grad * slope).astype(BF)
    back_part = by_lane(dot(hid_grad, w_in, ((1,), (1,))).astype(BF))
    back_parts = exchange(back_part.reshape(ex_count, dp_count, -1), "expert")
    back_sum = jnp.sum(back_parts.astype(F32), axis=0).astype(BF)

    moved_in = exchange(slot_in, "dp")
    all_in = by_image(lax.all_gather(moved_in, "expert", axis=0, tiled=True))
    grad_w_out = dot(act, all_grad, ((0,), (0,))).astype(BF)
    grad_w_in = dot(all_in, hid_grad, ((0,), (0,))).astype(BF)

    slot_out = exchange(out_sum, "dp")
    slot_back = exchange(back_sum, "dp")

    grads, router_part = [], 0.0
    for b in range(images):
        lanes = slice(b * width, (b + 1) * width)
        comb_grad = dot(slot_out[:, lanes], grad_out[b], ((1,), (1,)))
        disp_grad = dot(slot_back[:, lanes], tokens[b], ((1,), (1,)))
        through_comb = comb[b] * (comb_grad - jnp.sum(comb[b] * comb_grad, axis=0, keepdims=True))
        through_disp = disp[b] * (disp_grad - jnp.sum(disp[b] * disp_grad, axis=1, keepdims=True))
        logit_grad = (through_comb + through_disp).astype(BF)
        left = jnp.concatenate([disp_b[b], logit_grad], axis=0)
        right = jnp.concatenate([slot_back[:, lanes], router], axis=0)
        grads.append(dot(left, right, ((0,), (0,))).astype(BF))
        router_part = router_part + dot(logit_grad, tokens[b], ((1,), (0,)))
    grad_x = jnp.stack(grads)

    row = jnp.sum(exchange(router_part, "dp"), axis=0, keepdims=True)
    rows = exchange(jnp.broadcast_to(row[None], (ex_count, 1, width)), "expert")
    row = jnp.sum(rows, axis=0, keepdims=True)
    grad_router = exchange(jnp.broadcast_to(row, (dp_count, 1, width)), "dp").reshape(slots, width)
    return grad_x, grad_router, grad_w_in[None], grad_w_out[None]


def solution(mesh):
    return jax.shard_map(
        on_device,
        mesh=mesh,
        in_specs=(
            P(("dp", "expert"), None, None),
            P(("dp", "expert"), None, None),
            P(("dp", "expert"), None, None),
            P(),
            P("dp", None, "expert"),
            P("dp", None, "expert"),
            P("dp", "expert", None),
        ),
        out_specs=(
            P(("dp", "expert"), None, None),
            P(),
            P("dp", None, "expert"),
            P("dp", "expert", None),
        ),
        check_vma=False,
    )
```

```python
import functools

import jax
import jax.numpy as jnp
from jax import lax
from jax.experimental import pallas as pl
from jax.experimental.pallas import tpu as pltpu
from jax.sharding import PartitionSpec as P

BF = jnp.bfloat16
F32 = jnp.float32
MIB = 1024 * 1024
MOST = 60 * MIB


def gelu_slope(value):
    cdf = 0.5 * (1.0 + jax.scipy.special.erf(value * 0.7071067811865476))
    density = jnp.exp(-0.5 * value * value) * 0.3989422804014327
    return cdf + value * density


def dot(a, b, dims):
    return lax.dot_general(a, b, (dims, ((), ())), preferred_element_type=F32)


def softmax(scores, axis):
    over = jnp.exp(scores - jnp.max(scores, axis=axis, keepdims=True))
    return over / jnp.sum(over, axis=axis, keepdims=True)


def exchange(blocks, axis):
    return lax.all_to_all(blocks, axis, split_axis=0, concat_axis=0, tiled=True)


def after(value, *others):
    return lax.optimization_barrier((value,) + others)[0]


def kernel_call(kernel, inputs, outputs, flops=0, moved=0, scratch=(), vmem=16 * MIB):
    place = {
        "v": pl.BlockSpec(memory_space=pltpu.VMEM),
        "h": pl.BlockSpec(memory_space=pltpu.HBM),
        "r": pl.BlockSpec(memory_space=pltpu.HBM),
        "s": pl.BlockSpec(memory_space=pltpu.SMEM),
    }

    def run(*operands):
        n_in, n_out = len(operands), len(outputs)
        fetched = [i for i in range(n_in) if inputs[i] == "h"]
        stored = [i for i in range(n_out) if outputs[i][0] == "h"]
        staged = [pltpu.VMEM(operands[i].shape, operands[i].dtype) for i in fetched]
        staged += [pltpu.VMEM(outputs[i][1].shape, outputs[i][1].dtype) for i in stored]
        sems = [pltpu.SemaphoreType.DMA((len(staged),))] if staged else []

        def body(*refs):
            ins, outs = list(refs[:n_in]), list(refs[n_in : n_in + n_out])
            extra = list(refs[n_in + n_out :])
            buffers = extra[: len(staged)]
            sem = extra[len(staged)] if staged else None
            rest = extra[len(staged) + len(sems) :]
            copies = []
            for j, i in enumerate(fetched):
                copies.append(pltpu.make_async_copy(ins[i], buffers[j], sem.at[j]))
                copies[-1].start()
                ins[i] = buffers[j]
            for copy in copies:
                copy.wait()
            targets = [outs[i] for i in stored]
            for j, i in enumerate(stored):
                outs[i] = buffers[len(fetched) + j]
            kernel(*ins, *outs, *rest)
            copies = []
            for j, target in enumerate(targets):
                at = len(fetched) + j
                copies.append(pltpu.make_async_copy(buffers[at], target, sem.at[at]))
                copies[-1].start()
            for copy in copies:
                copy.wait()

        return pl.pallas_call(
            body,
            out_shape=tuple(o[1] for o in outputs),
            in_specs=[place[flag] for flag in inputs],
            out_specs=tuple(place[o[0]] for o in outputs),
            scratch_shapes=staged + sems + list(scratch),
            compiler_params=pltpu.CompilerParams(vmem_limit_bytes=vmem),
            cost_estimate=pl.CostEstimate(flops=flops, bytes_accessed=moved, transcendentals=0),
        )(*operands)

    return run


def shuffle(slots, pieces, back):
    total = slots * pieces
    row = lax.broadcasted_iota(jnp.int32, (total, total), 1 if back else 0)
    col = lax.broadcasted_iota(jnp.int32, (total, total), 0 if back else 1)
    return ((row % pieces) * slots + row // pieces == col).astype(BF)


def pack(rows, width):
    half = width // 2
    stack = jnp.concatenate([r[:, h * half : (h + 1) * half] for r in rows for h in range(2)], axis=0)
    return dot(shuffle(rows[0].shape[0], 2 * len(rows), False), stack, ((1,), (0,))).astype(BF)


def unpack(packed, slots):
    pieces = packed.shape[0] // slots
    stack = dot(shuffle(slots, pieces, True), packed, ((1,), (0,))).astype(BF)
    part = [stack[p * slots : (p + 1) * slots] for p in range(pieces)]
    return [jnp.concatenate(part[p : p + 2], axis=1) for p in range(0, pieces, 2)]


def fetch(pairs, sems):
    copies = [pltpu.make_async_copy(src, dst, sems.at[i]) for i, (src, dst) in enumerate(pairs)]
    for copy in copies:
        copy.start()
    return copies


def halves(src, dst, b):
    rows = src.shape[1] // 2
    return [(src.at[b, pl.ds(h * rows, rows)], dst.at[b, pl.ds(h * rows, rows)]) for h in range(2)]


def slots_kernel(logits_in, dy_in, tokens_in, out_ref, logits, dy, tokens, sems):
    images = dy.shape[0]
    pairs = [(logits_in, logits)]
    for src, dst in ((dy_in, dy), (tokens_in, tokens)):
        for b in range(images):
            pairs += halves(src, dst, b)
    copies = fetch(pairs, sems)
    copies[0].wait()
    rows = []
    for axis, values in ((0, dy), (1, tokens)):
        for b in range(images):
            at = 1 + 2 * (axis * images + b)
            weights = softmax(logits[b], axis).astype(BF)
            copies[at].wait()
            copies[at + 1].wait()
            rows.append(dot(weights, values[b], ((1,), (0,))).astype(BF))
    out_ref[...] = pack(rows, rows[0].shape[1])


def hidden_kernel(dp_count, ex_count, me_ref, fc1_ref, w_ref, act_ref, *refs):
    slope_refs, out_refs = refs[:2], refs[2:]
    total = fc1_ref.shape[0]
    images = total // (dp_count * ex_count)
    group = dp_count * images
    block = 2 * group
    me = me_ref[0]
    for c in range(total // block):
        at = lax.broadcasted_iota(jnp.int32, (block, total), 0) + c * block
        owner = lax.bitwise_xor(at // group, jnp.full(at.shape, me, jnp.int32))
        source = (at % dp_count) * (ex_count * images) + owner * images + (at // dp_count) % images
        pick = (source == lax.broadcasted_iota(jnp.int32, (block, total), 1)).astype(BF)
        pre = dot(pick, fc1_ref[...], ((1,), (0,)))
        cdf = 0.5 * (1.0 + lax.erf(pre * 0.7071067811865476))
        density = jnp.exp(-0.5 * pre * pre) * 0.3989422804014327
        act = (pre * cdf).astype(BF)
        act_ref[c * block : (c + 1) * block, :] = act
        slope_refs[c // 2][(c % 2) * block : (c % 2 + 1) * block, :] = (cdf + pre * density).astype(BF)
        out = dot(act, w_ref[...], ((1,), (0,))).astype(BF)
        out_refs[2 * c][...] = out[:group]
        out_refs[2 * c + 1][...] = out[group:]


def back_kernel(*refs):
    blocks, (slope_ref, w_out_ref, w_in_ref, hid_ref), outs = refs[:4], refs[4:8], refs[8:]
    group = blocks[0].shape[0]
    for c in range(0, 4, 2):
        rows = slice(c * group, (c + 2) * group)
        grad = jnp.concatenate([blocks[c][...], blocks[c + 1][...]], axis=0)
        hid = (dot(grad, w_out_ref[...], ((1,), (1,))) * slope_ref[rows, :].astype(F32)).astype(BF)
        hid_ref[rows, :] = hid
        back = dot(hid, w_in_ref[...], ((1,), (1,))).astype(BF)
        outs[c][...] = back[:group]
        outs[c + 1][...] = back[group:]


def weight_out_kernel(act_ref, *refs):
    grad = jnp.concatenate([r[...] for r in refs[:-1]], axis=0)
    for c in range(0, act_ref.shape[1], 128):
        cols = slice(c, c + 128)
        refs[-1][cols, :] = dot(act_ref[:, cols], grad, ((0,), (0,))).astype(BF)


def weight_in_kernel(me_ref, all_ref, hid_a_ref, hid_b_ref, out_ref):
    me = me_ref[0]
    group = all_ref.shape[1]
    rows = jnp.concatenate([all_ref[lax.bitwise_xor(me, jnp.int32(k))] for k in range(all_ref.shape[0])], axis=0)
    hid = jnp.concatenate([hid_a_ref[...], hid_b_ref[...]], axis=0)
    for c in range(0, rows.shape[1], 256):
        cols = slice(c, c + 256)
        out_ref[cols, :] = dot(rows[:, cols], hid, ((0,), (0,))).astype(BF)


def unpack_kernel(slots, moved_ref, grad_ref, in_ref):
    rows = unpack(moved_ref[...], slots)
    count = len(rows) // 2
    for b in range(count):
        at = slice(b * slots, (b + 1) * slots)
        grad_ref[at, :] = rows[b]
        in_ref[at, :] = rows[count + b]


def sum_kernel(images, *refs):
    out_ref = refs[-1]
    each = (len(refs) - 1) // 2
    slots = refs[0].shape[0] // images
    sums = []
    for first in (0, each):
        total = refs[first][...].astype(F32)
        for ref in refs[first + 1 : first + each]:
            total = total + ref[...].astype(F32)
        total = total.astype(BF)
        sums += [total[b * slots : (b + 1) * slots] for b in range(images)]
    out_ref[...] = pack(sums, refs[0].shape[1])


def logits_kernel(owners, moved_ref, logits_in, tokens_in, dy_in, disp_ref, grad_ref, back_ref, router_ref, logits, tokens, dy, sems):
    images, slots, _ = logits.shape
    pairs = [(logits_in, logits)]
    for src, dst in ((dy_in, dy), (tokens_in, tokens)):
        for b in range(images):
            pairs += halves(src, dst, b)
    copies = fetch(pairs, sems)
    rows = unpack(moved_ref[...], slots)
    copies[0].wait()
    parts = []
    for b in range(images):
        comb = softmax(logits[b], 0)
        disp = softmax(logits[b], 1)
        back_ref[b] = rows[images + b]
        for axis in range(2):
            at = 1 + 2 * (axis * images + b)
            copies[at].wait()
            copies[at + 1].wait()
        comb_grad = dot(rows[b], dy[b], ((1,), (1,)))
        disp_grad = dot(rows[images + b], tokens[b], ((1,), (1,)))
        through_comb = comb * (comb_grad - jnp.sum(comb * comb_grad, axis=0, keepdims=True))
        through_disp = disp * (disp_grad - jnp.sum(disp * disp_grad, axis=1, keepdims=True))
        logit_grad = (through_comb + through_disp).astype(BF)
        disp_ref[b] = disp.astype(BF)
        grad_ref[b] = logit_grad
        parts.append(dot(logit_grad, tokens[b], ((1,), (0,))))
    part = sum(parts[1:], parts[0])
    count, half = slots // owners, part.shape[1] // 2
    for k in range(owners):
        for h in range(2):
            at = (2 * k + h) * count
            router_ref[at : at + count, :] = part[k * count : (k + 1) * count, h * half : (h + 1) * half]


def total_kernel(parts_ref, out_ref):
    total = parts_ref[0].astype(F32)
    for k in range(1, parts_ref.shape[0]):
        total = total + parts_ref[k].astype(F32)
    total = total.astype(out_ref.dtype)
    for k in range(out_ref.shape[0]):
        out_ref[k] = total


def rows_kernel(parts_ref, out_ref):
    owners, count, half = parts_ref.shape
    count = count // 2
    for k in range(owners):
        for h in range(2):
            out_ref[k * count : (k + 1) * count, h * half : (h + 1) * half] = parts_ref[k, h * count : (h + 1) * count, :]


def tokens_kernel(disp_ref, grad_ref, back_ref, router_ref, out_ref):
    for b in range(out_ref.shape[0]):
        rows = dot(disp_ref[b], back_ref[b], ((0,), (0,)))
        out_ref[b] = (rows + dot(grad_ref[b], router_ref[...], ((0,), (0,)))).astype(BF)


def on_device(tokens, grad_out, logits, router, fc1_out, w_in, w_out):
    images, slots, count = logits.shape
    width = tokens.shape[2]
    dp_count = lax.axis_size("dp")
    ex_count = lax.axis_size("expert")
    group = dp_count * images
    total = group * ex_count
    w_in, w_out, fc1 = w_in[0], w_out[0], fc1_out[0]
    small = 2 * images * slots * count * width

    def shape(dtype, *dims):
        return jax.ShapeDtypeStruct(dims, dtype)

    fetched = [
        pltpu.VMEM(logits.shape, F32),
        pltpu.VMEM(tokens.shape, BF),
        pltpu.VMEM(tokens.shape, BF),
        pltpu.SemaphoreType.DMA((1 + 4 * images,)),
    ]
    packed_shape = shape(BF, slots * 4 * images, width // 2)

    def swap(packed):
        return exchange(packed.reshape(dp_count, -1, width // 2), "dp").reshape(packed.shape)

    (packed,) = kernel_call(slots_kernel, "rrr", [("v", packed_shape)], 2 * small, 2 * tokens.nbytes, fetched, MOST)(
        logits, grad_out, tokens
    )
    moved = swap(packed)

    hidden = fc1.shape[1]
    big = 2 * total * width * hidden
    me = lax.axis_index("expert").astype(jnp.int32).reshape(1)
    block = shape(BF, group, width)

    def to_peer(value, k):
        return lax.ppermute(value, "expert", [(i, i ^ k) for i in range(ex_count)])

    act, slope_a, slope_b, *out_part = kernel_call(
        functools.partial(hidden_kernel, dp_count, ex_count),
        "svv",
        [("v", shape(BF, total, hidden))] + [("v", shape(BF, total // 2, hidden))] * 2 + [("v", block)] * ex_count,
        2 * big,
        10 * total * hidden,
        vmem=MOST,
    )(me, after(fc1, packed), w_out)
    own_grad, moved_in = kernel_call(
        functools.partial(unpack_kernel, slots), "v", [("v", block), ("v", block)], small, total * width
    )(after(moved, *out_part))
    grad_blocks = [own_grad] + [to_peer(own_grad, k) for k in range(1, ex_count)]
    out_blocks = [out_part[0]]
    for k in range(1, ex_count):
        out_blocks.append(to_peer(out_part[k], k))

    hid, back_part = [], []
    for h, slope in enumerate((slope_a, slope_b)):
        hid_half, *part = kernel_call(
            back_kernel,
            "v" * 7,
            [("v", shape(BF, total // 2, hidden))] + [("v", block)] * 4,
            big,
            5 * total * hidden,
        )(*grad_blocks[4 * h : 4 * h + 4], slope, w_out, w_in)
        hid.append(hid_half)
        back_part += part
    back_blocks = [back_part[0]] + [to_peer(back_part[k], k) for k in range(1, ex_count)]

    (both,) = kernel_call(
        functools.partial(sum_kernel, images),
        "v" * (2 * ex_count),
        [("v", packed_shape)],
        total * width,
        2 * total * width,
    )(*out_blocks, *back_blocks)
    moved_both = swap(both)
    all_in = lax.all_gather(after(moved_in, both), "expert", axis=0, tiled=False)

    half = width // 2
    count_rows = 2 * slots // ex_count
    disp_b, logit_grad, back_rows, router_part = kernel_call(
        functools.partial(logits_kernel, ex_count),
        "vrrr",
        [
            ("v", shape(BF, images, slots, count)),
            ("v", shape(BF, images, slots, count)),
            ("v", shape(BF, images, slots, width)),
            ("v", shape(F32, 2 * slots, half)),
        ],
        3 * small,
        2 * tokens.nbytes,
        fetched,
        20 * MIB,
    )(moved_both, logits, tokens, grad_out)
    (grad_x,) = kernel_call(tokens_kernel, "vvvv", [("v", shape(BF, *tokens.shape))], 2 * small, tokens.nbytes)(
        disp_b, logit_grad, back_rows, router
    )
    (grad_w_out,) = kernel_call(
        weight_out_kernel, "v" * (ex_count + 1), [("v", shape(BF, hidden, width))], big, 10 * total * hidden
    )(act, *grad_blocks)
    (grad_w_in,) = kernel_call(
        weight_in_kernel, "svvv", [("v", shape(BF, width, hidden))], big, 10 * total * hidden
    )(me, all_in, *hid)

    parts = exchange(router_part.reshape(ex_count, count_rows, half), "expert")
    (spread,) = kernel_call(total_kernel, "v", [("v", shape(BF, dp_count, count_rows, half))], small, tokens.nbytes)(parts)
    parts = after(exchange(spread, "dp"), grad_x, grad_w_out)
    (spread,) = kernel_call(total_kernel, "v", [("v", shape(F32, ex_count, count_rows, half))], small, tokens.nbytes)(parts)
    parts = exchange(spread, "expert")
    (grad_router,) = kernel_call(rows_kernel, "v", [("v", shape(F32, slots, width))], small, tokens.nbytes)(
        after(parts, grad_w_in)
    )
    return grad_x, grad_router, grad_w_in[None], grad_w_out[None]


def solution(mesh):
    return jax.shard_map(
        on_device,
        mesh=mesh,
        in_specs=(
            P(("dp", "expert"), None, None),
            P(("dp", "expert"), None, None),
            P(("dp", "expert"), None, None),
            P(),
            P("dp", None, "expert"),
            P("dp", None, "expert"),
            P("dp", "expert", None),
        ),
        out_specs=(
            P(("dp", "expert"), None, None),
            P(),
            P("dp", None, "expert"),
            P("dp", "expert", None),
        ),
        check_vma=False,
    )
```

```python
import functools

import jax
import jax.numpy as jnp
from jax import lax
from jax.experimental import pallas as pl
from jax.experimental.pallas import tpu as pltpu
from jax.sharding import PartitionSpec as P

BF = jnp.bfloat16
F32 = jnp.float32
MIB = 1024 * 1024
MOST = 60 * MIB
RING = 4


def gelu_slope(value):
    cdf = 0.5 * (1.0 + jax.scipy.special.erf(value * 0.7071067811865476))
    density = jnp.exp(-0.5 * value * value) * 0.3989422804014327
    return cdf + value * density


def dot(a, b, dims):
    return lax.dot_general(a, b, (dims, ((), ())), preferred_element_type=F32)


def softmax(scores, axis):
    over = jnp.exp(scores - jnp.max(scores, axis=axis, keepdims=True))
    return over / jnp.sum(over, axis=axis, keepdims=True)


def exchange(blocks, axis):
    return lax.all_to_all(blocks, axis, split_axis=0, concat_axis=0, tiled=True)


def after(value, *others):
    return lax.optimization_barrier((value,) + others)[0]


def kernel_call(kernel, inputs, outputs, flops=0, moved=0, scratch=(), vmem=16 * MIB):
    place = {
        "v": pl.BlockSpec(memory_space=pltpu.VMEM),
        "h": pl.BlockSpec(memory_space=pltpu.HBM),
        "r": pl.BlockSpec(memory_space=pltpu.HBM),
        "s": pl.BlockSpec(memory_space=pltpu.SMEM),
    }

    def run(*operands):
        n_in, n_out = len(operands), len(outputs)
        fetched = [i for i in range(n_in) if inputs[i] == "h"]
        stored = [i for i in range(n_out) if outputs[i][0] == "h"]
        staged = [pltpu.VMEM(operands[i].shape, operands[i].dtype) for i in fetched]
        staged += [pltpu.VMEM(outputs[i][1].shape, outputs[i][1].dtype) for i in stored]
        sems = [pltpu.SemaphoreType.DMA((len(staged),))] if staged else []

        def body(*refs):
            ins, outs = list(refs[:n_in]), list(refs[n_in : n_in + n_out])
            extra = list(refs[n_in + n_out :])
            buffers = extra[: len(staged)]
            sem = extra[len(staged)] if staged else None
            rest = extra[len(staged) + len(sems) :]
            copies = []
            for j, i in enumerate(fetched):
                copies.append(pltpu.make_async_copy(ins[i], buffers[j], sem.at[j]))
                copies[-1].start()
                ins[i] = buffers[j]
            for copy in copies:
                copy.wait()
            targets = [outs[i] for i in stored]
            for j, i in enumerate(stored):
                outs[i] = buffers[len(fetched) + j]
            kernel(*ins, *outs, *rest)
            copies = []
            for j, target in enumerate(targets):
                at = len(fetched) + j
                copies.append(pltpu.make_async_copy(buffers[at], target, sem.at[at]))
                copies[-1].start()
            for copy in copies:
                copy.wait()

        return pl.pallas_call(
            body,
            out_shape=tuple(o[1] for o in outputs),
            in_specs=[place[flag] for flag in inputs],
            out_specs=tuple(place[o[0]] for o in outputs),
            scratch_shapes=staged + sems + list(scratch),
            compiler_params=pltpu.CompilerParams(vmem_limit_bytes=vmem),
            cost_estimate=pl.CostEstimate(flops=flops, bytes_accessed=moved, transcendentals=0),
        )(*operands)

    return run


def shuffle(slots, pieces, back):
    total = slots * pieces
    row = lax.broadcasted_iota(jnp.int32, (total, total), 1 if back else 0)
    col = lax.broadcasted_iota(jnp.int32, (total, total), 0 if back else 1)
    return ((row % pieces) * slots + row // pieces == col).astype(BF)


def pack(rows, width):
    half = width // 2
    stack = jnp.concatenate([r[:, h * half : (h + 1) * half] for r in rows for h in range(2)], axis=0)
    return dot(shuffle(rows[0].shape[0], 2 * len(rows), False), stack, ((1,), (0,))).astype(BF)


def unpack(packed, slots):
    pieces = packed.shape[0] // slots
    stack = dot(shuffle(slots, pieces, True), packed, ((1,), (0,))).astype(BF)
    part = [stack[p * slots : (p + 1) * slots] for p in range(pieces)]
    return [jnp.concatenate(part[p : p + 2], axis=1) for p in range(0, pieces, 2)]


def fetch(pairs, sems):
    copies = [pltpu.make_async_copy(src, dst, sems.at[i]) for i, (src, dst) in enumerate(pairs)]
    for copy in copies:
        copy.start()
    return copies


def halves(src, dst, b):
    rows = src.shape[1] // 2
    return [(src.at[b, pl.ds(h * rows, rows)], dst.at[b, pl.ds(h * rows, rows)]) for h in range(2)]


def slots_kernel(logits_in, dy_in, tokens_in, out_ref, logits, dy, tokens, sems):
    images = dy.shape[0]
    pairs = [(logits_in, logits)]
    for src, dst in ((dy_in, dy), (tokens_in, tokens)):
        for b in range(images):
            pairs += halves(src, dst, b)
    copies = fetch(pairs, sems)
    copies[0].wait()
    rows = []
    for axis, values in ((0, dy), (1, tokens)):
        for b in range(images):
            at = 1 + 2 * (axis * images + b)
            weights = softmax(logits[b], axis).astype(BF)
            copies[at].wait()
            copies[at + 1].wait()
            rows.append(dot(weights, values[b], ((1,), (0,))).astype(BF))
    out_ref[...] = pack(rows, rows[0].shape[1])


def hidden_kernel(dp_count, ex_count, me_ref, fc1_ref, w_ref, act_ref, *refs):
    slope_refs, out_refs = refs[:2], refs[2:]
    total = fc1_ref.shape[0]
    images = total // (dp_count * ex_count)
    group = dp_count * images
    block = 2 * group
    me = me_ref[0]
    for c in range(total // block):
        at = lax.broadcasted_iota(jnp.int32, (block, total), 0) + c * block
        row = at // group
        owner = (row + me) % RING + RING * ((row // RING + me // RING) % 2)
        source = (at % dp_count) * (ex_count * images) + owner * images + (at // dp_count) % images
        pick = (source == lax.broadcasted_iota(jnp.int32, (block, total), 1)).astype(BF)
        pre = dot(pick, fc1_ref[...], ((1,), (0,)))
        cdf = 0.5 * (1.0 + lax.erf(pre * 0.7071067811865476))
        density = jnp.exp(-0.5 * pre * pre) * 0.3989422804014327
        act = (pre * cdf).astype(BF)
        act_ref[c * block : (c + 1) * block, :] = act
        slope_refs[c // 2][(c % 2) * block : (c % 2 + 1) * block, :] = (cdf + pre * density).astype(BF)
        out = dot(act, w_ref[...], ((1,), (0,))).astype(BF)
        for h in range(2):
            far, step = (2 * c + h) // RING, (2 * c + h) % RING
            out_refs[step][far * group : (far + 1) * group, :] = out[h * group : (h + 1) * group]


def back_kernel(*refs):
    blocks, (slope_ref, w_out_ref, w_in_ref, hid_ref), outs = refs[:4], refs[4:8], refs[8:]
    group = blocks[0].shape[0]
    for c in range(0, 4, 2):
        rows = slice(c * group, (c + 2) * group)
        grad = jnp.concatenate([blocks[c][...], blocks[c + 1][...]], axis=0)
        hid = (dot(grad, w_out_ref[...], ((1,), (1,))) * slope_ref[rows, :].astype(F32)).astype(BF)
        hid_ref[rows, :] = hid
        back = dot(hid, w_in_ref[...], ((1,), (1,))).astype(BF)
        outs[c][...] = back[:group]
        outs[c + 1][...] = back[group:]


def weight_out_kernel(act_ref, *refs):
    grad = jnp.concatenate([r[...] for r in refs[:-1]], axis=0)
    for c in range(0, act_ref.shape[1], 128):
        cols = slice(c, c + 128)
        refs[-1][cols, :] = dot(act_ref[:, cols], grad, ((0,), (0,))).astype(BF)


def weight_in_kernel(*refs):
    pairs, hid_refs, out_ref = refs[:RING], refs[RING : RING + 2], refs[-1]
    group = pairs[0].shape[0] // 2
    rows = jnp.concatenate([r[z * group : (z + 1) * group, :] for z in range(2) for r in pairs], axis=0)
    hid = jnp.concatenate([r[...] for r in hid_refs], axis=0)
    for c in range(0, rows.shape[1], 256):
        cols = slice(c, c + 256)
        out_ref[cols, :] = dot(rows[:, cols], hid, ((0,), (0,))).astype(BF)


def unpack_kernel(slots, moved_ref, grad_ref, in_ref):
    rows = unpack(moved_ref[...], slots)
    count = len(rows) // 2
    for b in range(count):
        at = slice(b * slots, (b + 1) * slots)
        grad_ref[at, :] = rows[b]
        in_ref[at, :] = rows[count + b]


def plane_kernel(*refs):
    far_ref, group = refs[4], refs[4].shape[0]
    both = refs[0].shape[0] > group

    def add(rows):
        total = refs[0][rows, :].astype(F32)
        for ref in refs[1:4]:
            total = total + ref[rows, :].astype(F32)
        return total

    far_ref[...] = add(slice(group, 2 * group) if both else slice(0, group)).astype(BF)
    if both:
        refs[5][...] = add(slice(0, group))


def sum_kernel(images, *refs):
    out_ref = refs[-1]
    slots = refs[0].shape[0] // images
    sums = []
    for parts in (refs[:2], refs[2:-1]):
        total = parts[0][...].astype(F32)
        for ref in parts[1:]:
            total = total + ref[...].astype(F32)
        total = total.astype(BF)
        sums += [total[b * slots : (b + 1) * slots] for b in range(images)]
    out_ref[...] = pack(sums, refs[0].shape[1])


def logits_kernel(owners, moved_ref, logits_in, tokens_in, dy_in, disp_ref, grad_ref, back_ref, router_ref, logits, tokens, dy, sems):
    images, slots, _ = logits.shape
    pairs = [(logits_in, logits)]
    for src, dst in ((dy_in, dy), (tokens_in, tokens)):
        for b in range(images):
            pairs += halves(src, dst, b)
    copies = fetch(pairs, sems)
    rows = unpack(moved_ref[...], slots)
    copies[0].wait()
    parts = []
    for b in range(images):
        comb = softmax(logits[b], 0)
        disp = softmax(logits[b], 1)
        back_ref[b] = rows[images + b]
        for axis in range(2):
            at = 1 + 2 * (axis * images + b)
            copies[at].wait()
            copies[at + 1].wait()
        comb_grad = dot(rows[b], dy[b], ((1,), (1,)))
        disp_grad = dot(rows[images + b], tokens[b], ((1,), (1,)))
        through_comb = comb * (comb_grad - jnp.sum(comb * comb_grad, axis=0, keepdims=True))
        through_disp = disp * (disp_grad - jnp.sum(disp * disp_grad, axis=1, keepdims=True))
        logit_grad = (through_comb + through_disp).astype(BF)
        disp_ref[b] = disp.astype(BF)
        grad_ref[b] = logit_grad
        parts.append(dot(logit_grad, tokens[b], ((1,), (0,))))
    part = sum(parts[1:], parts[0])
    count, half = slots // owners, part.shape[1] // 2
    for k in range(owners):
        for h in range(2):
            at = (2 * k + h) * count
            router_ref[at : at + count, :] = part[k * count : (k + 1) * count, h * half : (h + 1) * half]


def total_kernel(parts_ref, out_ref):
    total = parts_ref[0].astype(F32)
    for k in range(1, parts_ref.shape[0]):
        total = total + parts_ref[k].astype(F32)
    total = total.astype(out_ref.dtype)
    for k in range(out_ref.shape[0]):
        out_ref[k] = total


def rows_kernel(parts_ref, out_ref):
    owners, count, half = parts_ref.shape
    count = count // 2
    for k in range(owners):
        for h in range(2):
            out_ref[k * count : (k + 1) * count, h * half : (h + 1) * half] = parts_ref[k, h * count : (h + 1) * count, :]


def tokens_kernel(disp_ref, grad_ref, back_ref, router_ref, out_ref):
    for b in range(out_ref.shape[0]):
        rows = dot(disp_ref[b], back_ref[b], ((0,), (0,)))
        out_ref[b] = (rows + dot(grad_ref[b], router_ref[...], ((0,), (0,)))).astype(BF)


def on_device(tokens, grad_out, logits, router, fc1_out, w_in, w_out):
    images, slots, count = logits.shape
    width = tokens.shape[2]
    dp_count = lax.axis_size("dp")
    ex_count = lax.axis_size("expert")
    group = dp_count * images
    total = group * ex_count
    w_in, w_out, fc1 = w_in[0], w_out[0], fc1_out[0]
    small = 2 * images * slots * count * width

    def shape(dtype, *dims):
        return jax.ShapeDtypeStruct(dims, dtype)

    fetched = [
        pltpu.VMEM(logits.shape, F32),
        pltpu.VMEM(tokens.shape, BF),
        pltpu.VMEM(tokens.shape, BF),
        pltpu.SemaphoreType.DMA((1 + 4 * images,)),
    ]
    packed_shape = shape(BF, slots * 4 * images, width // 2)

    def swap(packed):
        return exchange(packed.reshape(dp_count, -1, width // 2), "dp").reshape(packed.shape)

    (packed,) = kernel_call(slots_kernel, "rrr", [("v", packed_shape)], 2 * small, 2 * tokens.nbytes, fetched, MOST)(
        logits, grad_out, tokens
    )
    moved = swap(packed)

    hidden = fc1.shape[1]
    big = 2 * total * width * hidden
    me = lax.axis_index("expert").astype(jnp.int32).reshape(1)
    block = shape(BF, group, width)

    def along(value, steps):
        return lax.ppermute(value, "expert", [(i, i // RING * RING + (i + steps) % RING) for i in range(ex_count)])

    def across(value):
        return lax.ppermute(value, "expert", [(i, (i + RING) % ex_count) for i in range(ex_count)])

    act, slope_a, slope_b, *out_part = kernel_call(
        functools.partial(hidden_kernel, dp_count, ex_count),
        "svv",
        [("v", shape(BF, total, hidden))] + [("v", shape(BF, total // 2, hidden))] * 2 + [("v", shape(BF, 2 * group, width))] * RING,
        2 * big,
        10 * total * hidden,
        vmem=MOST,
    )(me, after(fc1, packed), w_out)
    own_grad, moved_in = kernel_call(
        functools.partial(unpack_kernel, slots), "v", [("v", block), ("v", block)], small, total * width
    )(after(moved, *out_part))
    out_ring = [out_part[0], along(out_part[1], 1), None, along(out_part[3], 3)]
    ready = after(own_grad, out_ring[1], out_ring[3])
    near = [own_grad] + [along(ready, -d) for d in range(1, RING)]
    other = across(own_grad)
    far = [other] + [along(after(other, near[1]), -d) for d in range(1, RING)]
    grad_blocks = near + far
    out_ring[2] = along(after(out_part[2], *far), 2)

    hid, back_part = [], []
    for blocks, slope in ((near, slope_a), (far, slope_b)):
        hid_half, *part = kernel_call(
            back_kernel,
            "v" * 7,
            [("v", shape(BF, total // 2, hidden))] + [("v", block)] * RING,
            big,
            5 * total * hidden,
        )(*blocks, slope, w_out, w_in)
        hid.append(hid_half)
        back_part.append([part[0]] + [along(part[d], d) for d in range(1, RING)])

    (far_back,) = kernel_call(plane_kernel, "v" * RING, [("v", block)], total * width, total * width)(*back_part[1])
    far_back = across(far_back)
    far_out, near_out = kernel_call(
        plane_kernel, "v" * RING, [("v", block), ("v", shape(F32, group, width))], total * width, 2 * total * width
    )(*out_ring)
    far_out = across(far_out)

    other_in = across(after(moved_in, *far))
    (both,) = kernel_call(
        functools.partial(sum_kernel, images),
        "v" * (3 + RING),
        [("v", packed_shape)],
        total * width,
        2 * total * width,
    )(after(near_out, other_in), far_out, *back_part[0], far_back)
    in_pair = after(jnp.concatenate([moved_in, other_in], axis=0), both)
    in_pairs = [in_pair] + [along(in_pair, -d) for d in range(1, RING)]
    moved_both = swap(both)

    half = width // 2
    count_rows = 2 * slots // ex_count
    disp_b, logit_grad, back_rows, router_part = kernel_call(
        functools.partial(logits_kernel, ex_count),
        "vrrr",
        [
            ("h", shape(BF, images, slots, count)),
            ("h", shape(BF, images, slots, count)),
            ("h", shape(BF, images, slots, width)),
            ("v", shape(F32, 2 * slots, half)),
        ],
        3 * small,
        2 * tokens.nbytes,
        fetched,
        20 * MIB,
    )(moved_both, logits, tokens, grad_out)
    (grad_x,) = kernel_call(tokens_kernel, "vvvv", [("v", shape(BF, *tokens.shape))], 2 * small, tokens.nbytes)(
        disp_b, logit_grad, back_rows, router
    )
    (grad_w_out,) = kernel_call(
        weight_out_kernel, "v" * (ex_count + 1), [("v", shape(BF, hidden, width))], big, 10 * total * hidden
    )(act, *grad_blocks)
    (grad_w_in,) = kernel_call(
        weight_in_kernel, "v" * (RING + 2), [("v", shape(BF, width, hidden))], big, 10 * total * hidden
    )(*in_pairs, *hid)

    parts = exchange(router_part.reshape(ex_count, count_rows, half), "expert")
    (spread,) = kernel_call(total_kernel, "v", [("v", shape(BF, dp_count, count_rows, half))], small, tokens.nbytes)(parts)
    parts = after(exchange(spread, "dp"), grad_x, grad_w_out)
    (spread,) = kernel_call(total_kernel, "v", [("v", shape(F32, ex_count, count_rows, half))], small, tokens.nbytes)(parts)
    parts = exchange(spread, "expert")
    (grad_router,) = kernel_call(rows_kernel, "v", [("v", shape(F32, slots, width))], small, tokens.nbytes)(
        after(parts, grad_w_in)
    )
    return grad_x, grad_router, grad_w_in[None], grad_w_out[None]


def solution(mesh):
    return jax.shard_map(
        on_device,
        mesh=mesh,
        in_specs=(
            P(("dp", "expert"), None, None),
            P(("dp", "expert"), None, None),
            P(("dp", "expert"), None, None),
            P(),
            P("dp", None, "expert"),
            P("dp", None, "expert"),
            P("dp", "expert", None),
        ),
        out_specs=(
            P(("dp", "expert"), None, None),
            P(),
            P("dp", None, "expert"),
            P("dp", "expert", None),
        ),
        check_vma=False,
    )
```

```python
import functools

import jax
import jax.numpy as jnp
from jax import lax
from jax.experimental import pallas as pl
from jax.experimental.pallas import tpu as pltpu
from jax.sharding import PartitionSpec as P

BF = jnp.bfloat16
F32 = jnp.float32
MIB = 1024 * 1024
MOST = 60 * MIB
LANES = 384
RING = 4
ORDER = (0, 1, 3, 2)


def gelu_slope(value):
    cdf = 0.5 * (1.0 + jax.scipy.special.erf(value * 0.7071067811865476))
    density = jnp.exp(-0.5 * value * value) * 0.3989422804014327
    return cdf + value * density


def dot(a, b, dims):
    return lax.dot_general(a, b, (dims, ((), ())), preferred_element_type=F32)


def softmax(scores, axis):
    over = jnp.exp(scores - jnp.max(scores, axis=axis, keepdims=True))
    return over / jnp.sum(over, axis=axis, keepdims=True)


def exchange(blocks, axis):
    return lax.all_to_all(blocks, axis, split_axis=0, concat_axis=0, tiled=True)


def after(value, *others):
    return lax.optimization_barrier((value,) + others)[0]


def kernel_call(kernel, inputs, outputs, flops=0, moved=0, scratch=(), vmem=16 * MIB):
    place = {
        "v": pl.BlockSpec(memory_space=pltpu.VMEM),
        "h": pl.BlockSpec(memory_space=pltpu.HBM),
        "r": pl.BlockSpec(memory_space=pltpu.HBM),
        "s": pl.BlockSpec(memory_space=pltpu.SMEM),
    }

    def run(*operands):
        n_in, n_out = len(operands), len(outputs)
        fetched = [i for i in range(n_in) if inputs[i] == "h"]
        stored = [i for i in range(n_out) if outputs[i][0] == "h"]
        staged = [pltpu.VMEM(operands[i].shape, operands[i].dtype) for i in fetched]
        staged += [pltpu.VMEM(outputs[i][1].shape, outputs[i][1].dtype) for i in stored]
        sems = [pltpu.SemaphoreType.DMA((len(staged),))] if staged else []

        def body(*refs):
            ins, outs = list(refs[:n_in]), list(refs[n_in : n_in + n_out])
            extra = list(refs[n_in + n_out :])
            buffers = extra[: len(staged)]
            sem = extra[len(staged)] if staged else None
            rest = extra[len(staged) + len(sems) :]
            copies = []
            for j, i in enumerate(fetched):
                copies.append(pltpu.make_async_copy(ins[i], buffers[j], sem.at[j]))
                copies[-1].start()
                ins[i] = buffers[j]
            for copy in copies:
                copy.wait()
            targets = [outs[i] for i in stored]
            for j, i in enumerate(stored):
                outs[i] = buffers[len(fetched) + j]
            kernel(*ins, *outs, *rest)
            copies = []
            for j, target in enumerate(targets):
                at = len(fetched) + j
                copies.append(pltpu.make_async_copy(buffers[at], target, sem.at[at]))
                copies[-1].start()
            for copy in copies:
                copy.wait()

        return pl.pallas_call(
            body,
            out_shape=tuple(o[1] for o in outputs),
            in_specs=[place[flag] for flag in inputs],
            out_specs=tuple(place[o[0]] for o in outputs),
            scratch_shapes=staged + sems + list(scratch),
            compiler_params=pltpu.CompilerParams(vmem_limit_bytes=vmem),
            cost_estimate=pl.CostEstimate(flops=flops, bytes_accessed=moved, transcendentals=0),
        )(*operands)

    return run


def shuffle(slots, pieces, back):
    total = slots * pieces
    row = lax.broadcasted_iota(jnp.int32, (total, total), 1 if back else 0)
    col = lax.broadcasted_iota(jnp.int32, (total, total), 0 if back else 1)
    return ((row % pieces) * slots + row // pieces == col).astype(BF)


def pack(rows, width):
    half = width // 2
    stack = jnp.concatenate([r[:, h * half : (h + 1) * half] for r in rows for h in range(2)], axis=0)
    return dot(shuffle(rows[0].shape[0], 2 * len(rows), False), stack, ((1,), (0,))).astype(BF)


def unpack(packed, slots):
    pieces = packed.shape[0] // slots
    stack = dot(shuffle(slots, pieces, True), packed, ((1,), (0,))).astype(BF)
    part = [stack[p * slots : (p + 1) * slots] for p in range(pieces)]
    return [jnp.concatenate(part[p : p + 2], axis=1) for p in range(0, pieces, 2)]


def fetch(pairs, sems):
    copies = [pltpu.make_async_copy(src, dst, sems.at[i]) for i, (src, dst) in enumerate(pairs)]
    for copy in copies:
        copy.start()
    return copies


def halves(src, dst, b):
    rows = src.shape[1] // 2
    return [(src.at[b, pl.ds(h * rows, rows)], dst.at[b, pl.ds(h * rows, rows)]) for h in range(2)]


def slots_kernel(logits_in, dy_in, tokens_in, out_ref, logits, dy, tokens, sems):
    images = dy.shape[0]
    pairs = [(logits_in, logits)]
    for src, dst in ((dy_in, dy), (tokens_in, tokens)):
        for b in range(images):
            pairs += halves(src, dst, b)
    copies = fetch(pairs, sems)
    copies[0].wait()
    rows = []
    for axis, values in ((0, dy), (1, tokens)):
        for b in range(images):
            at = 1 + 2 * (axis * images + b)
            weights = softmax(logits[b], axis).astype(BF)
            copies[at].wait()
            copies[at + 1].wait()
            rows.append(dot(weights, values[b], ((1,), (0,))).astype(BF))
    out_ref[...] = pack(rows, rows[0].shape[1])


def hidden_kernel(dp_count, ex_count, me_ref, fc1_ref, w_ref, act_ref, *refs):
    slope_refs, out_refs = refs[:2], refs[2:]
    total = fc1_ref.shape[0]
    images = total // (dp_count * ex_count)
    group = dp_count * images
    block = 2 * group
    me = me_ref[0]
    for c, steps in enumerate(ORDER):
        at = lax.broadcasted_iota(jnp.int32, (block, total), 0)
        owner = (steps + me) % RING + RING * ((at // group + me // RING) % 2)
        source = (at % dp_count) * (ex_count * images) + owner * images + (at // dp_count) % images
        pick = (source == lax.broadcasted_iota(jnp.int32, (block, total), 1)).astype(BF)
        pre = dot(pick, fc1_ref[...], ((1,), (0,)))
        cdf = 0.5 * (1.0 + lax.erf(pre * 0.7071067811865476))
        density = jnp.exp(-0.5 * pre * pre) * 0.3989422804014327
        act = (pre * cdf).astype(BF)
        act_ref[c * block : (c + 1) * block, :] = act
        slope = (cdf + pre * density).astype(BF)
        if c < RING - 1:
            slope_refs[0][c * block : (c + 1) * block, :] = slope
        else:
            slope_refs[1][...] = slope
        out_refs[c][...] = dot(act, w_ref[...], ((1,), (0,))).astype(BF)


def back_kernel(*refs):
    count = (len(refs) - 4) // 2
    blocks, (slope_ref, w_out_ref, w_in_ref, hid_ref), outs = refs[:count], refs[count : count + 4], refs[count + 4 :]
    block = blocks[0].shape[0]
    for c in range(count):
        rows = slice(c * block, (c + 1) * block)
        grad = dot(blocks[c][...], w_out_ref[...], ((1,), (1,)))
        hid = (grad * slope_ref[rows, :].astype(F32)).astype(BF)
        hid_ref[rows, :] = hid
        outs[c][...] = dot(hid, w_in_ref[...], ((1,), (1,))).astype(BF)


def join_kernel(a_ref, b_ref, out_ref):
    group = a_ref.shape[0]
    out_ref[:group, :] = a_ref[...]
    out_ref[group:, :] = b_ref[...]


def weight_out_kernel(act_ref, *refs):
    grad = jnp.concatenate([r[...] for r in refs[:-1]], axis=0)
    for c in range(0, act_ref.shape[1], 128):
        cols = slice(c, c + 128)
        refs[-1][cols, :] = dot(act_ref[:, cols], grad, ((0,), (0,))).astype(BF)


def weight_in_kernel(*refs):
    pairs, hid_refs, out_ref = refs[:RING], refs[RING : RING + 2], refs[-1]
    rows = jnp.concatenate([r[...] for r in pairs], axis=0)
    hid = jnp.concatenate([r[...] for r in hid_refs], axis=0)
    for c in range(0, rows.shape[1], 256):
        cols = slice(c, c + 256)
        out_ref[cols, :] = dot(rows[:, cols], hid, ((0,), (0,))).astype(BF)


def unpack_kernel(slots, moved_ref, grad_ref, in_ref):
    rows = unpack(moved_ref[...], slots)
    count = len(rows) // 2
    for b in range(count):
        at = slice(b * slots, (b + 1) * slots)
        grad_ref[at, :] = rows[b]
        in_ref[at, :] = rows[count + b]


def plane_kernel(*refs):
    near_ref, far_ref = refs[RING:]
    group = far_ref.shape[0]

    def add(rows):
        total = refs[0][rows, :].astype(F32)
        for ref in refs[1:RING]:
            total = total + ref[rows, :].astype(F32)
        return total

    near_ref[...] = add(slice(0, group))
    far_ref[...] = add(slice(group, 2 * group)).astype(BF)


def sum_kernel(images, *refs):
    out_ref = refs[-1]
    slots = refs[0].shape[0] // images
    sums = []
    for parts in (refs[:2], refs[2:-1]):
        total = parts[0][...].astype(F32)
        for ref in parts[1:]:
            total = total + ref[...].astype(F32)
        total = total.astype(BF)
        sums += [total[b * slots : (b + 1) * slots] for b in range(images)]
    out_ref[...] = pack(sums, refs[0].shape[1])


def logits_kernel(owners, moved_ref, logits_in, tokens_in, dy_in, disp_ref, grad_ref, back_ref, router_ref, logits, tokens, dy, sems):
    images, slots, _ = logits.shape
    pairs = [(logits_in, logits)]
    for src, dst in ((dy_in, dy), (tokens_in, tokens)):
        for b in range(images):
            pairs += halves(src, dst, b)
    copies = fetch(pairs, sems)
    rows = unpack(moved_ref[...], slots)
    copies[0].wait()
    parts = []
    for b in range(images):
        comb = softmax(logits[b], 0)
        disp = softmax(logits[b], 1)
        back_ref[b] = rows[images + b]
        for axis in range(2):
            at = 1 + 2 * (axis * images + b)
            copies[at].wait()
            copies[at + 1].wait()
        comb_grad = dot(rows[b], dy[b], ((1,), (1,)))
        disp_grad = dot(rows[images + b], tokens[b], ((1,), (1,)))
        through_comb = comb * (comb_grad - jnp.sum(comb * comb_grad, axis=0, keepdims=True))
        through_disp = disp * (disp_grad - jnp.sum(disp * disp_grad, axis=1, keepdims=True))
        logit_grad = (through_comb + through_disp).astype(BF)
        disp_ref[b] = disp.astype(BF)
        grad_ref[b] = logit_grad
        parts.append(dot(logit_grad, tokens[b], ((1,), (0,))))
    part = sum(parts[1:], parts[0])
    for p in range(owners):
        for at, slot, lanes in pieces(slots // owners, part.shape[1]):
            router_ref[p, at : at + 1, : lanes.stop - lanes.start] = part[p * slots // owners + slot][None, lanes]
            if lanes.stop - lanes.start < router_ref.shape[2]:
                router_ref[p, at : at + 1, lanes.stop - lanes.start :] = jnp.zeros(
                    (1, router_ref.shape[2] - lanes.stop + lanes.start), F32
                )


def pieces(count, width):
    each = -(-width // LANES)
    return [
        (slot * each + q, slot, slice(q * LANES, min(width, (q + 1) * LANES))) for slot in range(count) for q in range(each)
    ]


def total_kernel(parts_ref, out_ref):
    total = parts_ref[0].astype(F32)
    for k in range(1, parts_ref.shape[0]):
        total = total + parts_ref[k].astype(F32)
    total = total.astype(out_ref.dtype)
    for k in range(out_ref.shape[0]):
        out_ref[k] = total


def rows_kernel(parts_ref, out_ref):
    count = out_ref.shape[0] // parts_ref.shape[0]
    for p in range(parts_ref.shape[0]):
        for at, slot, lanes in pieces(count, out_ref.shape[1]):
            row = p * count + slot
            out_ref[row : row + 1, lanes] = parts_ref[p, at : at + 1, : lanes.stop - lanes.start]


def tokens_kernel(disp_ref, grad_ref, back_ref, router_ref, out_ref):
    for b in range(out_ref.shape[0]):
        rows = dot(disp_ref[b], back_ref[b], ((0,), (0,)))
        out_ref[b] = (rows + dot(grad_ref[b], router_ref[...], ((0,), (0,)))).astype(BF)


def on_device(tokens, grad_out, logits, router, fc1_out, w_in, w_out):
    images, slots, count = logits.shape
    width = tokens.shape[2]
    dp_count = lax.axis_size("dp")
    ex_count = lax.axis_size("expert")
    group = dp_count * images
    total = group * ex_count
    w_in, w_out, fc1 = w_in[0], w_out[0], fc1_out[0]
    small = 2 * images * slots * count * width

    def shape(dtype, *dims):
        return jax.ShapeDtypeStruct(dims, dtype)

    fetched = [
        pltpu.VMEM(logits.shape, F32),
        pltpu.VMEM(tokens.shape, BF),
        pltpu.VMEM(tokens.shape, BF),
        pltpu.SemaphoreType.DMA((1 + 4 * images,)),
    ]
    packed_shape = shape(BF, slots * 4 * images, width // 2)

    def swap(packed):
        return exchange(packed.reshape(dp_count, -1, width // 2), "dp").reshape(packed.shape)

    (packed,) = kernel_call(slots_kernel, "rrr", [("v", packed_shape)], 2 * small, 2 * tokens.nbytes, fetched, MOST)(
        logits, grad_out, tokens
    )
    moved = swap(packed)

    hidden = fc1.shape[1]
    big = 2 * total * width * hidden
    me = lax.axis_index("expert").astype(jnp.int32).reshape(1)
    block = shape(BF, group, width)
    pair = 2 * group

    def along(value, steps):
        return lax.ppermute(value, "expert", [(i, i // RING * RING + (i + steps) % RING) for i in range(ex_count)])

    def across(value):
        return lax.ppermute(value, "expert", [(i, (i + RING) % ex_count) for i in range(ex_count)])

    act, slope_a, slope_b, *out_part = kernel_call(
        functools.partial(hidden_kernel, dp_count, ex_count),
        "svv",
        [("v", shape(BF, total, hidden)), ("v", shape(BF, total - pair, hidden)), ("v", shape(BF, pair, hidden))]
        + [("v", shape(BF, pair, width))] * RING,
        2 * big,
        10 * total * hidden,
        vmem=MOST,
    )(me, after(fc1, packed), w_out)
    own_grad, moved_in = kernel_call(
        functools.partial(unpack_kernel, slots), "v", [("v", block), ("v", block)], small, total * width
    )(after(moved, *out_part))
    def joined(value, other):
        return kernel_call(join_kernel, "vv", [("v", shape(BF, pair, width))], pair * width, 4 * pair * width)(value, other)[0]

    def plane_sum(blocks):
        near, far = kernel_call(
            plane_kernel, "v" * RING, [("v", shape(F32, group, width)), ("v", block)], total * width, 2 * total * width
        )(*blocks)
        return near, across(far)

    out_ring = [out_part[0]] + [along(out_part[c], ORDER[c]) for c in range(1, RING - 1)]
    mine = joined(after(own_grad, *out_ring), across(own_grad))
    grads = [mine] + [along(mine, -steps) for steps in ORDER[1:]]
    out_ring.append(along(after(out_part[RING - 1], *grads), ORDER[RING - 1]))

    hid, back_ring = [], []
    for first, last, slope in ((0, RING - 1, slope_a), (RING - 1, RING, slope_b)):
        hid_rows, *part = kernel_call(
            back_kernel,
            "v" * (last - first + 3),
            [("v", shape(BF, pair * (last - first), hidden))] + [("v", shape(BF, pair, width))] * (last - first),
            2 * big * (last - first) // RING,
            5 * total * hidden,
        )(*grads[first:last], slope, w_out, w_in)
        hid.append(hid_rows)
        back_ring += [along(part[c - first], ORDER[c]) if c else part[c] for c in range(first, last)]

    near_out, far_out = plane_sum(out_ring)
    near_back, far_back = plane_sum(back_ring)
    other_in = across(after(moved_in, *grads))
    (both,) = kernel_call(
        functools.partial(sum_kernel, images), "vvvv", [("v", packed_shape)], total * width, 2 * total * width
    )(after(near_out, other_in), far_out, near_back, far_back)
    in_pair = joined(after(moved_in, both), other_in)
    in_pairs = [in_pair] + [along(in_pair, -steps) for steps in ORDER[1:]]
    moved_both = swap(both)

    teams = [[(2 * t + core) * ex_count + i for core in range(2) for i in range(ex_count)] for t in range(dp_count // 2)]
    peers = [[2 * t + core for t in range(dp_count // 2)] for core in range(2)]
    team = len(teams[0])
    rows = (slots // team) * -(-width // LANES)
    disp_b, logit_grad, back_rows, router_part = kernel_call(
        functools.partial(logits_kernel, team),
        "vrrr",
        [
            ("h", shape(BF, images, slots, count)),
            ("h", shape(BF, images, slots, count)),
            ("h", shape(BF, images, slots, width)),
            ("v", shape(F32, team, rows, LANES)),
        ],
        3 * small,
        2 * tokens.nbytes,
        fetched,
        20 * MIB,
    )(moved_both, logits, tokens, grad_out)
    (grad_x,) = kernel_call(tokens_kernel, "vvvv", [("v", shape(BF, *tokens.shape))], 2 * small, tokens.nbytes)(
        disp_b, logit_grad, back_rows, router
    )
    (grad_w_out,) = kernel_call(
        weight_out_kernel, "v" * (RING + 1), [("v", shape(BF, hidden, width))], big, 10 * total * hidden
    )(act, *grads)
    (grad_w_in,) = kernel_call(
        weight_in_kernel, "v" * (RING + 2), [("v", shape(BF, width, hidden))], big, 10 * total * hidden
    )(*in_pairs, *hid)

    def swap_rows(value, axes, groups):
        return lax.all_to_all(value, axes, split_axis=0, concat_axis=0, axis_index_groups=groups, tiled=True)

    def spread_sum(parts, dtype, count):
        return kernel_call(total_kernel, "v", [("v", shape(dtype, count, rows, LANES))], small, tokens.nbytes)(parts)[0]

    parts = after(swap_rows(router_part, ("dp", "expert"), teams), grad_w_out)
    parts = after(swap_rows(spread_sum(parts, BF, len(teams)), "dp", peers), grad_x)
    parts = swap_rows(spread_sum(parts, F32, team), ("dp", "expert"), teams)
    (grad_router,) = kernel_call(rows_kernel, "v", [("v", shape(F32, slots, width))], small, tokens.nbytes)(
        after(parts, grad_w_in)
    )
    return grad_x, grad_router, grad_w_in[None], grad_w_out[None]


def solution(mesh):
    return jax.shard_map(
        on_device,
        mesh=mesh,
        in_specs=(
            P(("dp", "expert"), None, None),
            P(("dp", "expert"), None, None),
            P(("dp", "expert"), None, None),
            P(),
            P("dp", None, "expert"),
            P("dp", None, "expert"),
            P("dp", "expert", None),
        ),
        out_specs=(
            P(("dp", "expert"), None, None),
            P(),
            P("dp", None, "expert"),
            P("dp", "expert", None),
        ),
        check_vma=False,
    )
```

```python
import functools

import jax
import jax.numpy as jnp
from jax import lax
from jax.experimental import pallas as pl
from jax.experimental.pallas import tpu as pltpu
from jax.sharding import PartitionSpec as P

BF = jnp.bfloat16
F32 = jnp.float32
MIB = 1024 * 1024
MOST = 60 * MIB
LANES = 384
RING = 4
ORDER = (0, 1, 3, 2)


def gelu_slope(value):
    cdf = 0.5 * (1.0 + jax.scipy.special.erf(value * 0.7071067811865476))
    density = jnp.exp(-0.5 * value * value) * 0.3989422804014327
    return cdf + value * density


def dot(a, b, dims):
    return lax.dot_general(a, b, (dims, ((), ())), preferred_element_type=F32)


def softmax(scores, axis):
    over = jnp.exp(scores - jnp.max(scores, axis=axis, keepdims=True))
    return over / jnp.sum(over, axis=axis, keepdims=True)


def exchange(blocks, axis):
    return lax.all_to_all(blocks, axis, split_axis=0, concat_axis=0, tiled=True)


def after(value, *others):
    return lax.optimization_barrier((value,) + others)[0]


def kernel_call(kernel, inputs, outputs, flops=0, moved=0, scratch=(), vmem=16 * MIB):
    place = {
        "v": pl.BlockSpec(memory_space=pltpu.VMEM),
        "h": pl.BlockSpec(memory_space=pltpu.HBM),
        "r": pl.BlockSpec(memory_space=pltpu.HBM),
        "s": pl.BlockSpec(memory_space=pltpu.SMEM),
    }

    def run(*operands):
        n_in, n_out = len(operands), len(outputs)
        fetched = [i for i in range(n_in) if inputs[i] == "h"]
        stored = [i for i in range(n_out) if outputs[i][0] == "h"]
        staged = [pltpu.VMEM(operands[i].shape, operands[i].dtype) for i in fetched]
        staged += [pltpu.VMEM(outputs[i][1].shape, outputs[i][1].dtype) for i in stored]
        sems = [pltpu.SemaphoreType.DMA((len(staged),))] if staged else []

        def body(*refs):
            ins, outs = list(refs[:n_in]), list(refs[n_in : n_in + n_out])
            extra = list(refs[n_in + n_out :])
            buffers = extra[: len(staged)]
            sem = extra[len(staged)] if staged else None
            rest = extra[len(staged) + len(sems) :]
            copies = []
            for j, i in enumerate(fetched):
                copies.append(pltpu.make_async_copy(ins[i], buffers[j], sem.at[j]))
                copies[-1].start()
                ins[i] = buffers[j]
            for copy in copies:
                copy.wait()
            targets = [outs[i] for i in stored]
            for j, i in enumerate(stored):
                outs[i] = buffers[len(fetched) + j]
            kernel(*ins, *outs, *rest)
            copies = []
            for j, target in enumerate(targets):
                at = len(fetched) + j
                copies.append(pltpu.make_async_copy(buffers[at], target, sem.at[at]))
                copies[-1].start()
            for copy in copies:
                copy.wait()

        return pl.pallas_call(
            body,
            out_shape=tuple(o[1] for o in outputs),
            in_specs=[place[flag] for flag in inputs],
            out_specs=tuple(place[o[0]] for o in outputs),
            scratch_shapes=staged + sems + list(scratch),
            compiler_params=pltpu.CompilerParams(vmem_limit_bytes=vmem),
            cost_estimate=pl.CostEstimate(flops=flops, bytes_accessed=moved, transcendentals=0),
        )(*operands)

    return run


def shuffle(slots, pieces, back):
    total = slots * pieces
    row = lax.broadcasted_iota(jnp.int32, (total, total), 1 if back else 0)
    col = lax.broadcasted_iota(jnp.int32, (total, total), 0 if back else 1)
    shift = pieces.bit_length() - 1
    if pieces == 1 << shift:
        return ((row & (pieces - 1)) * slots + (row >> shift) == col).astype(BF)
    return ((row % pieces) * slots + row // pieces == col).astype(BF)


def pack(rows, width):
    half = width // 2
    stack = jnp.concatenate([r[:, h * half : (h + 1) * half] for r in rows for h in range(2)], axis=0)
    return dot(shuffle(rows[0].shape[0], 2 * len(rows), False), stack, ((1,), (0,))).astype(BF)


def unpack(packed, slots):
    pieces = packed.shape[0] // slots
    stack = dot(shuffle(slots, pieces, True), packed, ((1,), (0,))).astype(BF)
    part = [stack[p * slots : (p + 1) * slots] for p in range(pieces)]
    return [jnp.concatenate(part[p : p + 2], axis=1) for p in range(0, pieces, 2)]


def fetch(pairs, sems):
    copies = [pltpu.make_async_copy(src, dst, sems.at[i]) for i, (src, dst) in enumerate(pairs)]
    for copy in copies:
        copy.start()
    return copies


def halves(src, dst, b):
    rows = src.shape[1] // 2
    return [(src.at[b, pl.ds(h * rows, rows)], dst.at[b, pl.ds(h * rows, rows)]) for h in range(2)]


def slots_kernel(logits_in, dy_in, tokens_in, out_ref, logits, dy, tokens, sems):
    images = dy.shape[0]
    pairs = [(logits_in, logits)]
    for src, dst in ((dy_in, dy), (tokens_in, tokens)):
        for b in range(images):
            pairs += halves(src, dst, b)
    copies = fetch(pairs, sems)
    copies[0].wait()
    rows = []
    for axis, values in ((0, dy), (1, tokens)):
        for b in range(images):
            at = 1 + 2 * (axis * images + b)
            weights = softmax(logits[b], axis).astype(BF)
            copies[at].wait()
            copies[at + 1].wait()
            rows.append(dot(weights, values[b], ((1,), (0,))).astype(BF))
    out_ref[...] = pack(rows, rows[0].shape[1])


def hidden_kernel(dp_count, ex_count, me_ref, fc1_ref, w_ref, act_ref, *refs):
    slope_refs, out_refs = refs[:2], refs[2:]
    total = fc1_ref.shape[0]
    images = total // (dp_count * ex_count)
    group = dp_count * images
    block = 2 * group
    me = me_ref[0]
    for c, steps in enumerate(ORDER):
        at = lax.broadcasted_iota(jnp.int32, (block, total), 0)
        owner = (steps + me) % RING + RING * ((at // group + me // RING) % 2)
        source = (at % dp_count) * (ex_count * images) + owner * images + (at // dp_count) % images
        pick = (source == lax.broadcasted_iota(jnp.int32, (block, total), 1)).astype(BF)
        pre = dot(pick, fc1_ref[...], ((1,), (0,)))
        cdf = 0.5 * (1.0 + lax.erf(pre * 0.7071067811865476))
        density = jnp.exp(-0.5 * pre * pre) * 0.3989422804014327
        act = (pre * cdf).astype(BF)
        act_ref[c * block : (c + 1) * block, :] = act
        slope = (cdf + pre * density).astype(BF)
        if c < RING - 1:
            slope_refs[0][c * block : (c + 1) * block, :] = slope
        else:
            slope_refs[1][...] = slope
        out_refs[c][...] = dot(act, w_ref[...], ((1,), (0,))).astype(BF)


def back_kernel(*refs):
    count = (len(refs) - 4) // 2
    blocks, (slope_ref, w_out_ref, w_in_ref, hid_ref), outs = refs[:count], refs[count : count + 4], refs[count + 4 :]
    block = blocks[0].shape[0]
    for c in range(count):
        rows = slice(c * block, (c + 1) * block)
        grad = dot(blocks[c][...], w_out_ref[...], ((1,), (1,)))
        hid = (grad * slope_ref[rows, :].astype(F32)).astype(BF)
        hid_ref[rows, :] = hid
        outs[c][...] = dot(hid, w_in_ref[...], ((1,), (1,))).astype(BF)


def join_kernel(a_ref, b_ref, out_ref):
    group = a_ref.shape[0]
    out_ref[:group, :] = a_ref[...]
    out_ref[group:, :] = b_ref[...]


def weight_out_kernel(act_ref, *refs):
    grad = jnp.concatenate([r[...] for r in refs[:-1]], axis=0)
    for c in range(0, act_ref.shape[1], 128):
        cols = slice(c, c + 128)
        refs[-1][cols, :] = dot(act_ref[:, cols], grad, ((0,), (0,))).astype(BF)


def weight_in_kernel(*refs):
    pairs, hid_refs, out_ref = refs[:RING], refs[RING : RING + 2], refs[-1]
    rows = jnp.concatenate([r[...] for r in pairs], axis=0)
    hid = jnp.concatenate([r[...] for r in hid_refs], axis=0)
    for c in range(0, rows.shape[1], 256):
        cols = slice(c, c + 256)
        out_ref[cols, :] = dot(rows[:, cols], hid, ((0,), (0,))).astype(BF)


def unpack_kernel(slots, moved_ref, grad_ref, in_ref):
    rows = unpack(moved_ref[...], slots)
    count = len(rows) // 2
    for b in range(count):
        at = slice(b * slots, (b + 1) * slots)
        grad_ref[at, :] = rows[b]
        in_ref[at, :] = rows[count + b]


def plane_kernel(*refs):
    near_ref, far_ref = refs[RING:]
    group = far_ref.shape[0]

    def add(rows):
        total = refs[0][rows, :].astype(F32)
        for ref in refs[1:RING]:
            total = total + ref[rows, :].astype(F32)
        return total

    near_ref[...] = add(slice(0, group))
    far_ref[...] = add(slice(group, 2 * group)).astype(BF)


def sum_kernel(images, *refs):
    out_ref = refs[-1]
    slots = refs[0].shape[0] // images
    sums = []
    for parts in (refs[:2], refs[2:-1]):
        total = parts[0][...].astype(F32)
        for ref in parts[1:]:
            total = total + ref[...].astype(F32)
        total = total.astype(BF)
        sums += [total[b * slots : (b + 1) * slots] for b in range(images)]
    out_ref[...] = pack(sums, refs[0].shape[1])


def logits_kernel(owners, moved_ref, logits, tokens, dy, disp_ref, grad_ref, back_ref, router_ref):
    images, slots, _ = logits.shape
    rows = unpack(moved_ref[...], slots)
    parts = []
    for b in range(images):
        comb = softmax(logits[b], 0)
        disp = softmax(logits[b], 1)
        back_ref[b] = rows[images + b]
        comb_grad = dot(rows[b], dy[b], ((1,), (1,)))
        disp_grad = dot(rows[images + b], tokens[b], ((1,), (1,)))
        through_comb = comb * (comb_grad - jnp.sum(comb * comb_grad, axis=0, keepdims=True))
        through_disp = disp * (disp_grad - jnp.sum(disp * disp_grad, axis=1, keepdims=True))
        logit_grad = (through_comb + through_disp).astype(BF)
        disp_ref[b] = disp.astype(BF)
        grad_ref[b] = logit_grad
        parts.append(dot(logit_grad, tokens[b], ((1,), (0,))))
    part = sum(parts[1:], parts[0])
    count, width = slots // owners, part.shape[1]
    for q, lanes in enumerate(pieces(width)):
        size = lanes.stop - lanes.start
        for p in range(owners):
            router_ref[p, q * count : (q + 1) * count, :size] = part[p * count : (p + 1) * count, lanes]
            if size < LANES:
                router_ref[p, q * count : (q + 1) * count, size:] = jnp.zeros((count, LANES - size), F32)


def pieces(width):
    return [slice(at, min(width, at + LANES)) for at in range(0, width, LANES)]


def total_kernel(parts_ref, out_ref):
    total = parts_ref[0].astype(F32)
    for k in range(1, parts_ref.shape[0]):
        total = total + parts_ref[k].astype(F32)
    total = total.astype(out_ref.dtype)
    for k in range(out_ref.shape[0]):
        out_ref[k] = total


def rows_kernel(parts_ref, out_ref):
    count = out_ref.shape[0] // parts_ref.shape[0]
    for q, lanes in enumerate(pieces(out_ref.shape[1])):
        for p in range(parts_ref.shape[0]):
            rows = parts_ref[p, q * count : (q + 1) * count, : lanes.stop - lanes.start]
            out_ref[p * count : (p + 1) * count, lanes] = rows


def tokens_kernel(disp_ref, grad_ref, back_ref, router_ref, out_ref):
    for b in range(out_ref.shape[0]):
        rows = dot(disp_ref[b], back_ref[b], ((0,), (0,)))
        out_ref[b] = (rows + dot(grad_ref[b], router_ref[...], ((0,), (0,)))).astype(BF)


def on_device(tokens, grad_out, logits, router, fc1_out, w_in, w_out):
    images, slots, count = logits.shape
    width = tokens.shape[2]
    dp_count = lax.axis_size("dp")
    ex_count = lax.axis_size("expert")
    group = dp_count * images
    total = group * ex_count
    w_in, w_out, fc1 = w_in[0], w_out[0], fc1_out[0]
    small = 2 * images * slots * count * width

    def shape(dtype, *dims):
        return jax.ShapeDtypeStruct(dims, dtype)

    fetched = [
        pltpu.VMEM(logits.shape, F32),
        pltpu.VMEM(tokens.shape, BF),
        pltpu.VMEM(tokens.shape, BF),
        pltpu.SemaphoreType.DMA((1 + 4 * images,)),
    ]
    packed_shape = shape(BF, slots * 4 * images, width // 2)

    def swap(packed):
        return exchange(packed.reshape(dp_count, -1, width // 2), "dp").reshape(packed.shape)

    (packed,) = kernel_call(slots_kernel, "rrr", [("v", packed_shape)], 2 * small, 2 * tokens.nbytes, fetched, MOST)(
        logits, grad_out, tokens
    )
    moved = swap(packed)

    hidden = fc1.shape[1]
    big = 2 * total * width * hidden
    me = lax.axis_index("expert").astype(jnp.int32).reshape(1)
    block = shape(BF, group, width)
    pair = 2 * group

    def along(value, steps):
        return lax.ppermute(value, "expert", [(i, i // RING * RING + (i + steps) % RING) for i in range(ex_count)])

    def across(value):
        return lax.ppermute(value, "expert", [(i, (i + RING) % ex_count) for i in range(ex_count)])

    act, slope_a, slope_b, *out_part = kernel_call(
        functools.partial(hidden_kernel, dp_count, ex_count),
        "svv",
        [("v", shape(BF, total, hidden)), ("v", shape(BF, total - pair, hidden)), ("v", shape(BF, pair, hidden))]
        + [("v", shape(BF, pair, width))] * RING,
        2 * big,
        10 * total * hidden,
        vmem=MOST,
    )(me, after(fc1, packed), w_out)
    own_grad, moved_in = kernel_call(
        functools.partial(unpack_kernel, slots), "v", [("v", block), ("v", block)], small, total * width
    )(after(moved, *out_part))
    def joined(value, other):
        return kernel_call(join_kernel, "vv", [("v", shape(BF, pair, width))], pair * width, 4 * pair * width)(value, other)[0]

    def plane_sum(blocks):
        near, far = kernel_call(
            plane_kernel, "v" * RING, [("v", shape(F32, group, width)), ("v", block)], total * width, 2 * total * width
        )(*blocks)
        return near, across(far)

    out_ring = [out_part[0]] + [along(out_part[c], ORDER[c]) for c in range(1, RING - 1)]
    mine = joined(after(own_grad, *out_ring), across(own_grad))
    grads = [mine] + [along(mine, -steps) for steps in ORDER[1:]]
    out_ring.append(along(after(out_part[RING - 1], *grads), ORDER[RING - 1]))

    hid, back_ring = [], []
    for first, last, slope in ((0, RING - 1, slope_a), (RING - 1, RING, slope_b)):
        hid_rows, *part = kernel_call(
            back_kernel,
            "v" * (last - first + 3),
            [("v", shape(BF, pair * (last - first), hidden))] + [("v", shape(BF, pair, width))] * (last - first),
            2 * big * (last - first) // RING,
            5 * total * hidden,
        )(*grads[first:last], slope, w_out, w_in)
        hid.append(hid_rows)
        back_ring += [along(part[c - first], ORDER[c]) if c else part[c] for c in range(first, last)]

    near_out, far_out = plane_sum(out_ring)
    near_back, far_back = plane_sum(back_ring)
    other_in = across(after(moved_in, *grads))
    (grad_w_out,) = kernel_call(
        weight_out_kernel, "v" * (RING + 1), [("v", shape(BF, hidden, width))], big, 10 * total * hidden
    )(act, *grads)
    (both,) = kernel_call(
        functools.partial(sum_kernel, images), "vvvv", [("v", packed_shape)], total * width, 2 * total * width
    )(after(near_out, other_in, grad_w_out), far_out, near_back, far_back)
    in_pair = joined(after(moved_in, both), other_in)
    in_pairs = [in_pair] + [along(in_pair, -steps) for steps in ORDER[1:]]
    moved_both = swap(both)

    teams = [[(2 * t + core) * ex_count + i for core in range(2) for i in range(ex_count)] for t in range(dp_count // 2)]
    peers = [[2 * t + core for t in range(dp_count // 2)] for core in range(2)]
    team = len(teams[0])
    rows = (slots // team) * -(-width // LANES)
    disp_b, logit_grad, back_rows, router_part = kernel_call(
        functools.partial(logits_kernel, team),
        "vvvv",
        [
            ("h", shape(BF, images, slots, count)),
            ("h", shape(BF, images, slots, count)),
            ("h", shape(BF, images, slots, width)),
            ("v", shape(F32, team, rows, LANES)),
        ],
        3 * small,
        2 * tokens.nbytes,
        vmem=20 * MIB,
    )(moved_both, logits, tokens, grad_out)
    (grad_x,) = kernel_call(tokens_kernel, "vvvv", [("v", shape(BF, *tokens.shape))], 2 * small, tokens.nbytes)(
        disp_b, logit_grad, back_rows, router
    )
    (grad_w_in,) = kernel_call(
        weight_in_kernel, "v" * (RING + 2), [("v", shape(BF, width, hidden))], big, 10 * total * hidden
    )(*in_pairs, *hid)

    def swap_rows(value, axes, groups):
        return lax.all_to_all(value, axes, split_axis=0, concat_axis=0, axis_index_groups=groups, tiled=True)

    def spread_sum(parts, dtype, count):
        return kernel_call(total_kernel, "v", [("v", shape(dtype, count, rows, LANES))], small, tokens.nbytes)(parts)[0]

    parts = after(swap_rows(router_part, ("dp", "expert"), teams), grad_x)
    parts = after(swap_rows(spread_sum(parts, BF, len(teams)), "dp", peers), grad_w_out)
    parts = swap_rows(spread_sum(parts, F32, team), ("dp", "expert"), teams)
    (grad_router,) = kernel_call(rows_kernel, "v", [("v", shape(F32, slots, width))], small, tokens.nbytes)(
        after(parts, grad_w_in)
    )
    return grad_x, grad_router, grad_w_in[None], grad_w_out[None]


def solution(mesh):
    return jax.shard_map(
        on_device,
        mesh=mesh,
        in_specs=(
            P(("dp", "expert"), None, None),
            P(("dp", "expert"), None, None),
            P(("dp", "expert"), None, None),
            P(),
            P("dp", None, "expert"),
            P("dp", None, "expert"),
            P("dp", "expert", None),
        ),
        out_specs=(
            P(("dp", "expert"), None, None),
            P(),
            P("dp", None, "expert"),
            P("dp", "expert", None),
        ),
        check_vma=False,
    )
```

```python
import functools

import jax
import jax.numpy as jnp
from jax import lax
from jax.experimental import pallas as pl
from jax.experimental.pallas import tpu as pltpu
from jax.sharding import PartitionSpec as P

BF = jnp.bfloat16
F32 = jnp.float32
MIB = 1024 * 1024
MOST = 60 * MIB
LANES = 384
RING = 4
ORDER = (0, 1, 3, 2)


def gelu_slope(value):
    cdf = 0.5 * (1.0 + jax.scipy.special.erf(value * 0.7071067811865476))
    density = jnp.exp(-0.5 * value * value) * 0.3989422804014327
    return cdf + value * density


def dot(a, b, dims):
    return lax.dot_general(a, b, (dims, ((), ())), preferred_element_type=F32)


def softmax(scores, axis):
    over = jnp.exp(scores - jnp.max(scores, axis=axis, keepdims=True))
    return over / jnp.sum(over, axis=axis, keepdims=True)


def exchange(blocks, axis):
    return lax.all_to_all(blocks, axis, split_axis=0, concat_axis=0, tiled=True)


def after(value, *others):
    return lax.optimization_barrier((value,) + others)[0]


def kernel_call(kernel, inputs, outputs, flops=0, moved=0, scratch=(), vmem=16 * MIB):
    place = {
        "v": pl.BlockSpec(memory_space=pltpu.VMEM),
        "h": pl.BlockSpec(memory_space=pltpu.HBM),
        "r": pl.BlockSpec(memory_space=pltpu.HBM),
        "s": pl.BlockSpec(memory_space=pltpu.SMEM),
    }

    def run(*operands):
        n_in, n_out = len(operands), len(outputs)
        fetched = [i for i in range(n_in) if inputs[i] == "h"]
        stored = [i for i in range(n_out) if outputs[i][0] == "h"]
        staged = [pltpu.VMEM(operands[i].shape, operands[i].dtype) for i in fetched]
        staged += [pltpu.VMEM(outputs[i][1].shape, outputs[i][1].dtype) for i in stored]
        sems = [pltpu.SemaphoreType.DMA((len(staged),))] if staged else []

        def body(*refs):
            ins, outs = list(refs[:n_in]), list(refs[n_in : n_in + n_out])
            extra = list(refs[n_in + n_out :])
            buffers = extra[: len(staged)]
            sem = extra[len(staged)] if staged else None
            rest = extra[len(staged) + len(sems) :]
            copies = []
            for j, i in enumerate(fetched):
                copies.append(pltpu.make_async_copy(ins[i], buffers[j], sem.at[j]))
                copies[-1].start()
                ins[i] = buffers[j]
            for copy in copies:
                copy.wait()
            targets = [outs[i] for i in stored]
            for j, i in enumerate(stored):
                outs[i] = buffers[len(fetched) + j]
            kernel(*ins, *outs, *rest)
            copies = []
            for j, target in enumerate(targets):
                at = len(fetched) + j
                copies.append(pltpu.make_async_copy(buffers[at], target, sem.at[at]))
                copies[-1].start()
            for copy in copies:
                copy.wait()

        return pl.pallas_call(
            body,
            out_shape=tuple(o[1] for o in outputs),
            in_specs=[place[flag] for flag in inputs],
            out_specs=tuple(place[o[0]] for o in outputs),
            scratch_shapes=staged + sems + list(scratch),
            compiler_params=pltpu.CompilerParams(vmem_limit_bytes=vmem),
            cost_estimate=pl.CostEstimate(flops=flops, bytes_accessed=moved, transcendentals=0),
        )(*operands)

    return run


def shuffle(slots, pieces, back):
    total = slots * pieces
    row = lax.broadcasted_iota(jnp.int32, (total, total), 1 if back else 0)
    col = lax.broadcasted_iota(jnp.int32, (total, total), 0 if back else 1)
    shift = pieces.bit_length() - 1
    if pieces == 1 << shift:
        return ((row & (pieces - 1)) * slots + (row >> shift) == col).astype(BF)
    return ((row % pieces) * slots + row // pieces == col).astype(BF)


def pack(rows, width):
    half = width // 2
    stack = jnp.concatenate([r[:, h * half : (h + 1) * half] for r in rows for h in range(2)], axis=0)
    return dot(shuffle(rows[0].shape[0], 2 * len(rows), False), stack, ((1,), (0,))).astype(BF)


def unpack(packed, slots):
    pieces = packed.shape[0] // slots
    stack = dot(shuffle(slots, pieces, True), packed, ((1,), (0,))).astype(BF)
    part = [stack[p * slots : (p + 1) * slots] for p in range(pieces)]
    return [jnp.concatenate(part[p : p + 2], axis=1) for p in range(0, pieces, 2)]


def fetch(pairs, sems):
    copies = [pltpu.make_async_copy(src, dst, sems.at[i]) for i, (src, dst) in enumerate(pairs)]
    for copy in copies:
        copy.start()
    return copies


def halves(src, dst, b):
    rows = src.shape[1] // 2
    return [(src.at[b, pl.ds(h * rows, rows)], dst.at[b, pl.ds(h * rows, rows)]) for h in range(2)]


def slots_kernel(logits_in, dy_in, tokens_in, out_ref, logits, dy, tokens, sems):
    images = dy.shape[0]
    pairs = [(logits_in, logits)]
    for src, dst in ((dy_in, dy), (tokens_in, tokens)):
        for b in range(images):
            pairs += halves(src, dst, b)
    copies = fetch(pairs, sems)
    copies[0].wait()
    rows = []
    for axis, values in ((0, dy), (1, tokens)):
        for b in range(images):
            at = 1 + 2 * (axis * images + b)
            weights = softmax(logits[b], axis).astype(BF)
            copies[at].wait()
            copies[at + 1].wait()
            rows.append(dot(weights, values[b], ((1,), (0,))).astype(BF))
    out_ref[...] = pack(rows, rows[0].shape[1])


def hidden_kernel(dp_count, ex_count, me_ref, fc1_ref, w_ref, act_ref, *refs):
    slope_refs, out_refs = refs[:2], refs[2:]
    total = fc1_ref.shape[0]
    images = total // (dp_count * ex_count)
    group = dp_count * images
    block = 2 * group
    me = me_ref[0]
    for c, steps in enumerate(ORDER):
        at = lax.broadcasted_iota(jnp.int32, (block, total), 0)
        owner = (steps + me) % RING + RING * ((at // group + me // RING) % 2)
        source = (at % dp_count) * (ex_count * images) + owner * images + (at // dp_count) % images
        pick = (source == lax.broadcasted_iota(jnp.int32, (block, total), 1)).astype(BF)
        pre = dot(pick, fc1_ref[...], ((1,), (0,)))
        cdf = 0.5 * (1.0 + lax.erf(pre * 0.7071067811865476))
        density = jnp.exp(-0.5 * pre * pre) * 0.3989422804014327
        act = (pre * cdf).astype(BF)
        act_ref[c * block : (c + 1) * block, :] = act
        slope = (cdf + pre * density).astype(BF)
        if c < RING - 1:
            slope_refs[0][c * block : (c + 1) * block, :] = slope
        else:
            slope_refs[1][...] = slope
        out_refs[c][...] = dot(act, w_ref[...], ((1,), (0,))).astype(BF)


def back_kernel(*refs):
    count = (len(refs) - 4) // 2
    blocks, (slope_ref, w_out_ref, w_in_ref, hid_ref), outs = refs[:count], refs[count : count + 4], refs[count + 4 :]
    block = blocks[0].shape[0]
    for c in range(count):
        rows = slice(c * block, (c + 1) * block)
        grad = dot(blocks[c][...], w_out_ref[...], ((1,), (1,)))
        hid = (grad * slope_ref[rows, :].astype(F32)).astype(BF)
        hid_ref[rows, :] = hid
        outs[c][...] = dot(hid, w_in_ref[...], ((1,), (1,))).astype(BF)


def join_kernel(a_ref, b_ref, out_ref):
    group = a_ref.shape[0]
    out_ref[:group, :] = a_ref[...]
    out_ref[group:, :] = b_ref[...]


def weight_out_kernel(act_ref, *refs):
    grad = jnp.concatenate([r[...] for r in refs[:-1]], axis=0)
    for c in range(0, act_ref.shape[1], 128):
        cols = slice(c, c + 128)
        refs[-1][cols, :] = dot(act_ref[:, cols], grad, ((0,), (0,))).astype(BF)


def weight_in_kernel(*refs):
    pairs, hid_refs, out_ref = refs[:RING], refs[RING : RING + 2], refs[-1]
    rows = jnp.concatenate([r[...] for r in pairs], axis=0)
    hid = jnp.concatenate([r[...] for r in hid_refs], axis=0)
    for c in range(0, rows.shape[1], 256):
        cols = slice(c, c + 256)
        out_ref[cols, :] = dot(rows[:, cols], hid, ((0,), (0,))).astype(BF)


def unpack_kernel(slots, moved_ref, grad_ref, in_ref):
    rows = unpack(moved_ref[...], slots)
    count = len(rows) // 2
    for b in range(count):
        at = slice(b * slots, (b + 1) * slots)
        grad_ref[at, :] = rows[b]
        in_ref[at, :] = rows[count + b]


def plane_kernel(*refs):
    near_ref, far_ref = refs[RING:]
    group = far_ref.shape[0]

    def add(rows):
        total = refs[0][rows, :].astype(F32)
        for ref in refs[1:RING]:
            total = total + ref[rows, :].astype(F32)
        return total

    near_ref[...] = add(slice(0, group))
    far_ref[...] = add(slice(group, 2 * group)).astype(BF)


def sum_kernel(images, *refs):
    out_ref = refs[-1]
    slots = refs[0].shape[0] // images
    sums = []
    for parts in (refs[:2], refs[2:-1]):
        total = parts[0][...].astype(F32)
        for ref in parts[1:]:
            total = total + ref[...].astype(F32)
        total = total.astype(BF)
        sums += [total[b * slots : (b + 1) * slots] for b in range(images)]
    out_ref[...] = pack(sums, refs[0].shape[1])


def logits_kernel(owners, moved_ref, logits, tokens, dy, disp_ref, grad_ref, back_ref, router_ref):
    images, slots, _ = logits.shape
    rows = unpack(moved_ref[...], slots)
    parts = []
    for b in range(images):
        comb = softmax(logits[b], 0)
        disp = softmax(logits[b], 1)
        back_ref[b] = rows[images + b]
        comb_grad = dot(rows[b], dy[b], ((1,), (1,)))
        disp_grad = dot(rows[images + b], tokens[b], ((1,), (1,)))
        through_comb = comb * (comb_grad - jnp.sum(comb * comb_grad, axis=0, keepdims=True))
        through_disp = disp * (disp_grad - jnp.sum(disp * disp_grad, axis=1, keepdims=True))
        logit_grad = (through_comb + through_disp).astype(BF)
        disp_ref[b] = disp.astype(BF)
        grad_ref[b] = logit_grad
        parts.append(dot(logit_grad, tokens[b], ((1,), (0,))))
    part = sum(parts[1:], parts[0])
    count, width = slots // owners, part.shape[1]
    for q, lanes in enumerate(pieces(width)):
        size = lanes.stop - lanes.start
        for p in range(owners):
            router_ref[p, q * count : (q + 1) * count, :size] = part[p * count : (p + 1) * count, lanes]
            if size < LANES:
                router_ref[p, q * count : (q + 1) * count, size:] = jnp.zeros((count, LANES - size), F32)


def pieces(width):
    return [slice(at, min(width, at + LANES)) for at in range(0, width, LANES)]


def total_kernel(parts_ref, out_ref):
    total = parts_ref[0].astype(F32)
    for k in range(1, parts_ref.shape[0]):
        total = total + parts_ref[k].astype(F32)
    total = total.astype(out_ref.dtype)
    for k in range(out_ref.shape[0]):
        out_ref[k] = total


def rows_kernel(parts_ref, out_ref):
    count = out_ref.shape[0] // parts_ref.shape[0]
    for q, lanes in enumerate(pieces(out_ref.shape[1])):
        for p in range(parts_ref.shape[0]):
            rows = parts_ref[p, q * count : (q + 1) * count, : lanes.stop - lanes.start]
            out_ref[p * count : (p + 1) * count, lanes] = rows


def tokens_kernel(disp_ref, grad_ref, back_ref, router_ref, out_ref):
    for b in range(out_ref.shape[0]):
        rows = dot(disp_ref[b], back_ref[b], ((0,), (0,)))
        out_ref[b] = (rows + dot(grad_ref[b], router_ref[...], ((0,), (0,)))).astype(BF)


def on_device(tokens, grad_out, logits, router, fc1_out, w_in, w_out):
    images, slots, count = logits.shape
    width = tokens.shape[2]
    dp_count = lax.axis_size("dp")
    ex_count = lax.axis_size("expert")
    group = dp_count * images
    total = group * ex_count
    w_in, w_out, fc1 = w_in[0], w_out[0], fc1_out[0]
    small = 2 * images * slots * count * width

    def shape(dtype, *dims):
        return jax.ShapeDtypeStruct(dims, dtype)

    fetched = [
        pltpu.VMEM(logits.shape, F32),
        pltpu.VMEM(tokens.shape, BF),
        pltpu.VMEM(tokens.shape, BF),
        pltpu.SemaphoreType.DMA((1 + 4 * images,)),
    ]
    packed_shape = shape(BF, slots * 4 * images, width // 2)

    def swap(packed):
        return exchange(packed.reshape(dp_count, -1, width // 2), "dp").reshape(packed.shape)

    (packed,) = kernel_call(slots_kernel, "rrr", [("v", packed_shape)], 2 * small, 2 * tokens.nbytes, fetched, MOST)(
        logits, grad_out, tokens
    )
    moved = swap(packed)

    hidden = fc1.shape[1]
    big = 2 * total * width * hidden
    me = lax.axis_index("expert").astype(jnp.int32).reshape(1)
    block = shape(BF, group, width)
    pair = 2 * group

    def along(value, steps):
        return lax.ppermute(value, "expert", [(i, i // RING * RING + (i + steps) % RING) for i in range(ex_count)])

    def across(value):
        return lax.ppermute(value, "expert", [(i, (i + RING) % ex_count) for i in range(ex_count)])

    act, slope_a, slope_b, *out_part = kernel_call(
        functools.partial(hidden_kernel, dp_count, ex_count),
        "svv",
        [("v", shape(BF, total, hidden)), ("v", shape(BF, total - pair, hidden)), ("v", shape(BF, pair, hidden))]
        + [("v", shape(BF, pair, width))] * RING,
        2 * big,
        10 * total * hidden,
        vmem=MOST,
    )(me, after(fc1, packed), w_out)
    own_grad, moved_in = kernel_call(
        functools.partial(unpack_kernel, slots), "v", [("v", block), ("v", block)], small, total * width
    )(after(moved, *out_part))
    def joined(value, other):
        return kernel_call(join_kernel, "vv", [("v", shape(BF, pair, width))], pair * width, 4 * pair * width)(value, other)[0]

    def plane_sum(blocks):
        near, far = kernel_call(
            plane_kernel, "v" * RING, [("v", shape(F32, group, width)), ("v", block)], total * width, 2 * total * width
        )(*blocks)
        return near, across(far)

    out_ring = [out_part[0]] + [along(out_part[c], ORDER[c]) for c in range(1, RING - 1)]
    mine = joined(after(own_grad, *out_ring), across(own_grad))
    grads = [mine] + [along(mine, -steps) for steps in ORDER[1:]]
    out_ring.append(along(after(out_part[RING - 1], *grads), ORDER[RING - 1]))

    hid, back_ring = [], []
    for first, last, slope in ((0, RING - 1, slope_a), (RING - 1, RING, slope_b)):
        hid_rows, *part = kernel_call(
            back_kernel,
            "v" * (last - first + 3),
            [("v", shape(BF, pair * (last - first), hidden))] + [("v", shape(BF, pair, width))] * (last - first),
            2 * big * (last - first) // RING,
            5 * total * hidden,
        )(*grads[first:last], slope, w_out, w_in)
        hid.append(hid_rows)
        back_ring += [along(part[c - first], ORDER[c]) if c else part[c] for c in range(first, last)]

    near_out, far_out = plane_sum(out_ring)
    near_back, far_back = plane_sum(back_ring)
    other_in = across(after(moved_in, *grads))
    (grad_w_out,) = kernel_call(
        weight_out_kernel, "v" * (RING + 1), [("v", shape(BF, hidden, width))], big, 10 * total * hidden
    )(act, *grads)
    (both,) = kernel_call(
        functools.partial(sum_kernel, images), "vvvv", [("v", packed_shape)], total * width, 2 * total * width
    )(after(near_out, other_in, grad_w_out), far_out, near_back, far_back)
    in_pair = joined(after(moved_in, both), other_in)
    in_pairs = [in_pair] + [along(in_pair, -steps) for steps in ORDER[1:]]
    moved_both = swap(both)

    teams = [[(2 * t + core) * ex_count + i for core in range(2) for i in range(ex_count)] for t in range(dp_count // 2)]
    peers = [[2 * t + core for t in range(dp_count // 2)] for core in range(2)]
    team = len(teams[0])
    rows = (slots // team) * -(-width // LANES)
    disp_b, logit_grad, back_rows, router_part = kernel_call(
        functools.partial(logits_kernel, team),
        "vvvv",
        [
            ("h", shape(BF, images, slots, count)),
            ("h", shape(BF, images, slots, count)),
            ("h", shape(BF, images, slots, width)),
            ("v", shape(F32, team, rows, LANES)),
        ],
        3 * small,
        2 * tokens.nbytes,
        vmem=20 * MIB,
    )(moved_both, logits, tokens, grad_out)
    (grad_x,) = kernel_call(tokens_kernel, "vvvv", [("v", shape(BF, *tokens.shape))], 2 * small, tokens.nbytes)(
        disp_b, logit_grad, back_rows, router
    )
    (grad_w_in,) = kernel_call(
        weight_in_kernel, "v" * (RING + 2), [("v", shape(BF, width, hidden))], big, 10 * total * hidden
    )(*in_pairs, *hid)

    def swap_rows(value, axes, groups):
        return lax.all_to_all(value, axes, split_axis=0, concat_axis=0, axis_index_groups=groups, tiled=True)

    def spread_sum(parts, dtype, count):
        return kernel_call(total_kernel, "v", [("v", shape(dtype, count, rows, LANES))], small, tokens.nbytes)(parts)[0]

    parts = swap_rows(router_part, ("dp", "expert"), teams)
    parts = after(swap_rows(spread_sum(parts, BF, len(teams)), "dp", peers), grad_x)
    parts = swap_rows(spread_sum(parts, F32, team), ("dp", "expert"), teams)
    (grad_router,) = kernel_call(rows_kernel, "v", [("v", shape(F32, slots, width))], small, tokens.nbytes)(
        after(parts, grad_w_in)
    )
    return grad_x, grad_router, grad_w_in[None], grad_w_out[None]


def solution(mesh):
    return jax.shard_map(
        on_device,
        mesh=mesh,
        in_specs=(
            P(("dp", "expert"), None, None),
            P(("dp", "expert"), None, None),
            P(("dp", "expert"), None, None),
            P(),
            P("dp", None, "expert"),
            P("dp", None, "expert"),
            P("dp", "expert", None),
        ),
        out_specs=(
            P(("dp", "expert"), None, None),
            P(),
            P("dp", None, "expert"),
            P("dp", "expert", None),
        ),
        check_vma=False,
    )
```

```python
import functools

import jax
import jax.numpy as jnp
from jax import lax
from jax.experimental import pallas as pl
from jax.experimental.pallas import tpu as pltpu
from jax.sharding import PartitionSpec as P

BF = jnp.bfloat16
F32 = jnp.float32
MIB = 1024 * 1024
MOST = 60 * MIB
LANES = 384
RING = 4
ORDER = (0, 1, 3, 2)


def gelu_slope(value):
    cdf = 0.5 * (1.0 + jax.scipy.special.erf(value * 0.7071067811865476))
    density = jnp.exp(-0.5 * value * value) * 0.3989422804014327
    return cdf + value * density


def dot(a, b, dims):
    return lax.dot_general(a, b, (dims, ((), ())), preferred_element_type=F32)


def softmax(scores, axis):
    over = jnp.exp(scores - jnp.max(scores, axis=axis, keepdims=True))
    return over / jnp.sum(over, axis=axis, keepdims=True)


def exchange(blocks, axis):
    return lax.all_to_all(blocks, axis, split_axis=0, concat_axis=0, tiled=True)


def after(value, *others):
    return lax.optimization_barrier((value,) + others)[0]


def kernel_call(kernel, inputs, outputs, flops=0, moved=0, scratch=(), vmem=16 * MIB):
    place = {
        "v": pl.BlockSpec(memory_space=pltpu.VMEM),
        "h": pl.BlockSpec(memory_space=pltpu.HBM),
        "r": pl.BlockSpec(memory_space=pltpu.HBM),
        "s": pl.BlockSpec(memory_space=pltpu.SMEM),
    }

    def run(*operands):
        n_in, n_out = len(operands), len(outputs)
        fetched = [i for i in range(n_in) if inputs[i] == "h"]
        stored = [i for i in range(n_out) if outputs[i][0] == "h"]
        staged = [pltpu.VMEM(operands[i].shape, operands[i].dtype) for i in fetched]
        staged += [pltpu.VMEM(outputs[i][1].shape, outputs[i][1].dtype) for i in stored]
        sems = [pltpu.SemaphoreType.DMA((len(staged),))] if staged else []

        def body(*refs):
            ins, outs = list(refs[:n_in]), list(refs[n_in : n_in + n_out])
            extra = list(refs[n_in + n_out :])
            buffers = extra[: len(staged)]
            sem = extra[len(staged)] if staged else None
            rest = extra[len(staged) + len(sems) :]
            copies = []
            for j, i in enumerate(fetched):
                copies.append(pltpu.make_async_copy(ins[i], buffers[j], sem.at[j]))
                copies[-1].start()
                ins[i] = buffers[j]
            for copy in copies:
                copy.wait()
            targets = [outs[i] for i in stored]
            for j, i in enumerate(stored):
                outs[i] = buffers[len(fetched) + j]
            kernel(*ins, *outs, *rest)
            copies = []
            for j, target in enumerate(targets):
                at = len(fetched) + j
                copies.append(pltpu.make_async_copy(buffers[at], target, sem.at[at]))
                copies[-1].start()
            for copy in copies:
                copy.wait()

        return pl.pallas_call(
            body,
            out_shape=tuple(o[1] for o in outputs),
            in_specs=[place[flag] for flag in inputs],
            out_specs=tuple(place[o[0]] for o in outputs),
            scratch_shapes=staged + sems + list(scratch),
            compiler_params=pltpu.CompilerParams(vmem_limit_bytes=vmem),
            cost_estimate=pl.CostEstimate(flops=flops, bytes_accessed=moved, transcendentals=0),
        )(*operands)

    return run


def shuffle(slots, pieces, back):
    total = slots * pieces
    row = lax.broadcasted_iota(jnp.int32, (total, total), 1 if back else 0)
    col = lax.broadcasted_iota(jnp.int32, (total, total), 0 if back else 1)
    shift = pieces.bit_length() - 1
    if pieces == 1 << shift:
        return ((row & (pieces - 1)) * slots + (row >> shift) == col).astype(BF)
    return ((row % pieces) * slots + row // pieces == col).astype(BF)


def pack(rows, width):
    half = width // 2
    stack = jnp.concatenate([r[:, h * half : (h + 1) * half] for r in rows for h in range(2)], axis=0)
    return dot(shuffle(rows[0].shape[0], 2 * len(rows), False), stack, ((1,), (0,))).astype(BF)


def unpack(packed, slots):
    pieces = packed.shape[0] // slots
    stack = dot(shuffle(slots, pieces, True), packed, ((1,), (0,))).astype(BF)
    part = [stack[p * slots : (p + 1) * slots] for p in range(pieces)]
    return [jnp.concatenate(part[p : p + 2], axis=1) for p in range(0, pieces, 2)]


def fetch(pairs, sems):
    copies = [pltpu.make_async_copy(src, dst, sems.at[i]) for i, (src, dst) in enumerate(pairs)]
    for copy in copies:
        copy.start()
    return copies


def halves(src, dst, b):
    rows = src.shape[1] // 2
    return [(src.at[b, pl.ds(h * rows, rows)], dst.at[b, pl.ds(h * rows, rows)]) for h in range(2)]


def slots_kernel(logits_in, dy_in, tokens_in, out_ref, logits, dy, tokens, sems):
    images = dy.shape[0]
    pairs = [(logits_in, logits)]
    for src, dst in ((dy_in, dy), (tokens_in, tokens)):
        for b in range(images):
            pairs += halves(src, dst, b)
    copies = fetch(pairs, sems)
    copies[0].wait()
    rows = []
    for axis, values in ((0, dy), (1, tokens)):
        for b in range(images):
            at = 1 + 2 * (axis * images + b)
            weights = softmax(logits[b], axis).astype(BF)
            copies[at].wait()
            copies[at + 1].wait()
            rows.append(dot(weights, values[b], ((1,), (0,))).astype(BF))
    out_ref[...] = pack(rows, rows[0].shape[1])


def hidden_kernel(dp_count, ex_count, me_ref, fc1_ref, w_ref, act_ref, *refs):
    slope_refs, out_refs = refs[:2], refs[2:]
    total = fc1_ref.shape[0]
    images = total // (dp_count * ex_count)
    group = dp_count * images
    block = 2 * group
    me = me_ref[0]
    for c, steps in enumerate(ORDER):
        at = lax.broadcasted_iota(jnp.int32, (block, total), 0)
        owner = (steps + me) % RING + RING * ((at // group + me // RING) % 2)
        source = (at % dp_count) * (ex_count * images) + owner * images + (at // dp_count) % images
        pick = (source == lax.broadcasted_iota(jnp.int32, (block, total), 1)).astype(BF)
        pre = dot(pick, fc1_ref[...], ((1,), (0,)))
        cdf = 0.5 * (1.0 + lax.erf(pre * 0.7071067811865476))
        density = jnp.exp(-0.5 * pre * pre) * 0.3989422804014327
        act = (pre * cdf).astype(BF)
        act_ref[c * block : (c + 1) * block, :] = act
        slope = (cdf + pre * density).astype(BF)
        if c < RING - 1:
            slope_refs[0][c * block : (c + 1) * block, :] = slope
        else:
            slope_refs[1][...] = slope
        out_refs[c][...] = dot(act, w_ref[...], ((1,), (0,))).astype(BF)


def back_kernel(*refs):
    count = (len(refs) - 4) // 2
    blocks, (slope_ref, w_out_ref, w_in_ref, hid_ref), outs = refs[:count], refs[count : count + 4], refs[count + 4 :]
    block = blocks[0].shape[0]
    for c in range(count):
        rows = slice(c * block, (c + 1) * block)
        grad = dot(blocks[c][...], w_out_ref[...], ((1,), (1,)))
        hid = (grad * slope_ref[rows, :].astype(F32)).astype(BF)
        hid_ref[rows, :] = hid
        outs[c][...] = dot(hid, w_in_ref[...], ((1,), (1,))).astype(BF)


def join_kernel(a_ref, b_ref, out_ref):
    group = a_ref.shape[0]
    out_ref[:group, :] = a_ref[...]
    out_ref[group:, :] = b_ref[...]


def weight_out_kernel(act_ref, *refs):
    grad = jnp.concatenate([r[...] for r in refs[:-1]], axis=0)
    for c in range(0, act_ref.shape[1], 128):
        cols = slice(c, c + 128)
        refs[-1][cols, :] = dot(act_ref[:, cols], grad, ((0,), (0,))).astype(BF)


def weight_in_kernel(*refs):
    pairs, hid_refs, out_ref = refs[:RING], refs[RING : RING + 2], refs[-1]
    rows = jnp.concatenate([r[...] for r in pairs], axis=0)
    hid = jnp.concatenate([r[...] for r in hid_refs], axis=0)
    for c in range(0, rows.shape[1], 256):
        cols = slice(c, c + 256)
        out_ref[cols, :] = dot(rows[:, cols], hid, ((0,), (0,))).astype(BF)


def unpack_kernel(slots, moved_ref, grad_ref, in_ref):
    rows = unpack(moved_ref[...], slots)
    count = len(rows) // 2
    for b in range(count):
        at = slice(b * slots, (b + 1) * slots)
        grad_ref[at, :] = rows[b]
        in_ref[at, :] = rows[count + b]


def plane_kernel(*refs):
    near_ref, far_ref = refs[RING:]
    group = far_ref.shape[0]

    def add(rows):
        total = refs[0][rows, :].astype(F32)
        for ref in refs[1:RING]:
            total = total + ref[rows, :].astype(F32)
        return total

    near_ref[...] = add(slice(0, group))
    far_ref[...] = add(slice(group, 2 * group)).astype(BF)


def sum_kernel(images, *refs):
    out_ref = refs[-1]
    slots = refs[0].shape[0] // images
    sums = []
    for parts in (refs[:2], refs[2:-1]):
        total = parts[0][...].astype(F32)
        for ref in parts[1:]:
            total = total + ref[...].astype(F32)
        total = total.astype(BF)
        sums += [total[b * slots : (b + 1) * slots] for b in range(images)]
    out_ref[...] = pack(sums, refs[0].shape[1])


def logits_kernel(owners, moved_ref, logits, tokens, dy, disp_ref, grad_ref, back_ref, router_ref):
    images, slots, _ = logits.shape
    rows = unpack(moved_ref[...], slots)
    parts = []
    for b in range(images):
        comb = softmax(logits[b], 0)
        disp = softmax(logits[b], 1)
        back_ref[b] = rows[images + b]
        comb_grad = dot(rows[b], dy[b], ((1,), (1,)))
        disp_grad = dot(rows[images + b], tokens[b], ((1,), (1,)))
        through_comb = comb * (comb_grad - jnp.sum(comb * comb_grad, axis=0, keepdims=True))
        through_disp = disp * (disp_grad - jnp.sum(disp * disp_grad, axis=1, keepdims=True))
        logit_grad = (through_comb + through_disp).astype(BF)
        disp_ref[b] = disp.astype(BF)
        grad_ref[b] = logit_grad
        parts.append(dot(logit_grad, tokens[b], ((1,), (0,))))
    part = sum(parts[1:], parts[0])
    count, width = slots // owners, part.shape[1]
    for q, lanes in enumerate(pieces(width)):
        size = lanes.stop - lanes.start
        for p in range(owners):
            router_ref[p, q * count : (q + 1) * count, :size] = part[p * count : (p + 1) * count, lanes]
            if size < LANES:
                router_ref[p, q * count : (q + 1) * count, size:] = jnp.zeros((count, LANES - size), F32)


def pieces(width):
    return [slice(at, min(width, at + LANES)) for at in range(0, width, LANES)]


def total_kernel(parts_ref, out_ref):
    total = parts_ref[0].astype(F32)
    for k in range(1, parts_ref.shape[0]):
        total = total + parts_ref[k].astype(F32)
    total = total.astype(out_ref.dtype)
    for k in range(out_ref.shape[0]):
        out_ref[k] = total


def rows_kernel(parts_ref, out_ref):
    count = out_ref.shape[0] // parts_ref.shape[0]
    for q, lanes in enumerate(pieces(out_ref.shape[1])):
        for p in range(parts_ref.shape[0]):
            rows = parts_ref[p, q * count : (q + 1) * count, : lanes.stop - lanes.start]
            out_ref[p * count : (p + 1) * count, lanes] = rows


def tokens_kernel(disp_ref, grad_ref, back_ref, router_ref, out_ref):
    for b in range(out_ref.shape[0]):
        rows = dot(disp_ref[b], back_ref[b], ((0,), (0,)))
        out_ref[b] = (rows + dot(grad_ref[b], router_ref[...], ((0,), (0,)))).astype(BF)


def on_device(tokens, grad_out, logits, router, fc1_out, w_in, w_out):
    images, slots, count = logits.shape
    width = tokens.shape[2]
    dp_count = lax.axis_size("dp")
    ex_count = lax.axis_size("expert")
    group = dp_count * images
    total = group * ex_count
    w_in, w_out, fc1 = w_in[0], w_out[0], fc1_out[0]
    small = 2 * images * slots * count * width

    def shape(dtype, *dims):
        return jax.ShapeDtypeStruct(dims, dtype)

    fetched = [
        pltpu.VMEM(logits.shape, F32),
        pltpu.VMEM(tokens.shape, BF),
        pltpu.VMEM(tokens.shape, BF),
        pltpu.SemaphoreType.DMA((1 + 4 * images,)),
    ]
    packed_shape = shape(BF, slots * 4 * images, width // 2)

    def swap(packed):
        return exchange(packed.reshape(dp_count, -1, width // 2), "dp").reshape(packed.shape)

    (packed,) = kernel_call(slots_kernel, "rrr", [("v", packed_shape)], 2 * small, 2 * tokens.nbytes, fetched, MOST)(
        logits, grad_out, tokens
    )
    moved = swap(packed)

    hidden = fc1.shape[1]
    big = 2 * total * width * hidden
    me = lax.axis_index("expert").astype(jnp.int32).reshape(1)
    block = shape(BF, group, width)
    pair = 2 * group

    def along(value, steps):
        return lax.ppermute(value, "expert", [(i, i // RING * RING + (i + steps) % RING) for i in range(ex_count)])

    def across(value):
        return lax.ppermute(value, "expert", [(i, (i + RING) % ex_count) for i in range(ex_count)])

    act, slope_a, slope_b, *out_part = kernel_call(
        functools.partial(hidden_kernel, dp_count, ex_count),
        "svv",
        [("v", shape(BF, total, hidden)), ("v", shape(BF, total - pair, hidden)), ("v", shape(BF, pair, hidden))]
        + [("v", shape(BF, pair, width))] * RING,
        2 * big,
        10 * total * hidden,
        vmem=MOST,
    )(me, after(fc1, packed), w_out)
    own_grad, moved_in = kernel_call(
        functools.partial(unpack_kernel, slots), "v", [("v", block), ("v", block)], small, total * width
    )(after(moved, *out_part))
    def joined(value, other):
        return kernel_call(join_kernel, "vv", [("v", shape(BF, pair, width))], pair * width, 4 * pair * width)(value, other)[0]

    def plane_sum(blocks):
        near, far = kernel_call(
            plane_kernel, "v" * RING, [("v", shape(F32, group, width)), ("v", block)], total * width, 2 * total * width
        )(*blocks)
        return near, across(far)

    out_ring = [out_part[0]] + [along(out_part[c], ORDER[c]) for c in range(1, RING - 1)]
    mine = joined(after(own_grad, *out_ring), across(own_grad))
    grads = [mine] + [along(mine, -steps) for steps in ORDER[1:]]

    hid, back_ring = [], []
    for first, last, slope in ((0, RING - 1, slope_a), (RING - 1, RING, slope_b)):
        hid_rows, *part = kernel_call(
            back_kernel,
            "v" * (last - first + 3),
            [("v", shape(BF, pair * (last - first), hidden))] + [("v", shape(BF, pair, width))] * (last - first),
            2 * big * (last - first) // RING,
            5 * total * hidden,
        )(*grads[first:last], slope, w_out, w_in)
        hid.append(hid_rows)
        back_ring += [along(part[c - first], ORDER[c]) if c else part[c] for c in range(first, last)]

    out_ring.append(along(after(out_part[RING - 1], hid[1]), ORDER[RING - 1]))
    near_out, far_out = plane_sum(out_ring)
    near_back, far_back = plane_sum(back_ring)
    other_in = across(after(moved_in, *grads))
    (grad_w_out,) = kernel_call(
        weight_out_kernel, "v" * (RING + 1), [("v", shape(BF, hidden, width))], big, 10 * total * hidden
    )(act, *grads)
    (both,) = kernel_call(
        functools.partial(sum_kernel, images), "vvvv", [("v", packed_shape)], total * width, 2 * total * width
    )(after(near_out, other_in, grad_w_out), far_out, near_back, far_back)
    in_pair = joined(after(moved_in, both), other_in)
    in_pairs = [in_pair] + [along(in_pair, -steps) for steps in ORDER[1:]]
    moved_both = swap(both)

    teams = [[(2 * t + core) * ex_count + i for core in range(2) for i in range(ex_count)] for t in range(dp_count // 2)]
    peers = [[2 * t + core for t in range(dp_count // 2)] for core in range(2)]
    team = len(teams[0])
    rows = (slots // team) * -(-width // LANES)
    disp_b, logit_grad, back_rows, router_part = kernel_call(
        functools.partial(logits_kernel, team),
        "vvvv",
        [
            ("h", shape(BF, images, slots, count)),
            ("h", shape(BF, images, slots, count)),
            ("h", shape(BF, images, slots, width)),
            ("v", shape(F32, team, rows, LANES)),
        ],
        3 * small,
        2 * tokens.nbytes,
        vmem=20 * MIB,
    )(moved_both, logits, tokens, grad_out)
    (grad_x,) = kernel_call(tokens_kernel, "vvvv", [("v", shape(BF, *tokens.shape))], 2 * small, tokens.nbytes)(
        disp_b, logit_grad, back_rows, router
    )
    (grad_w_in,) = kernel_call(
        weight_in_kernel, "v" * (RING + 2), [("v", shape(BF, width, hidden))], big, 10 * total * hidden
    )(*in_pairs, *hid)

    def swap_rows(value, axes, groups):
        return lax.all_to_all(value, axes, split_axis=0, concat_axis=0, axis_index_groups=groups, tiled=True)

    def spread_sum(parts, dtype, count):
        return kernel_call(total_kernel, "v", [("v", shape(dtype, count, rows, LANES))], small, tokens.nbytes)(parts)[0]

    parts = swap_rows(router_part, ("dp", "expert"), teams)
    parts = after(swap_rows(spread_sum(parts, BF, len(teams)), "dp", peers), grad_x)
    parts = swap_rows(spread_sum(parts, F32, team), ("dp", "expert"), teams)
    (grad_router,) = kernel_call(rows_kernel, "v", [("v", shape(F32, slots, width))], small, tokens.nbytes)(
        after(parts, grad_w_in)
    )
    return grad_x, grad_router, grad_w_in[None], grad_w_out[None]


def solution(mesh):
    return jax.shard_map(
        on_device,
        mesh=mesh,
        in_specs=(
            P(("dp", "expert"), None, None),
            P(("dp", "expert"), None, None),
            P(("dp", "expert"), None, None),
            P(),
            P("dp", None, "expert"),
            P("dp", None, "expert"),
            P("dp", "expert", None),
        ),
        out_specs=(
            P(("dp", "expert"), None, None),
            P(),
            P("dp", None, "expert"),
            P("dp", "expert", None),
        ),
        check_vma=False,
    )
```
